512 devices in a mesh: tm: 32 (over z_hi, y), chan: 16 (over z_lo, x, core).
Axes of the slice: x: 4, y: 8, z: 8 (z_hi: 4, z_lo: 2; z = z_hi * 2 + z_lo), core: 2. Of those that a mesh axis runs over, the one named last changes fastest.
Arguments:
- raw: bfloat16 [8192, 12288], P('tm', 'chan'), may hold values from -6 to 6
- taper: float32 [1024], replicated, may hold values from 0.1 to 1
- depth_owner: int32 [12288, 2], P('chan'), may hold values from 0 to 15, all different within a row; in each aligned block of 24 rows (0 to 23, 24 to 47, ...) at most 6 rows name the same one
- depth_slot: int32 [12288, 2], P('chan'), may hold values from 0 to 255
- intersection: int32 [12288, 2], P('chan'), may hold values from 1 to 100
Outputs:
- stacked: float32 [2, 4096, 1024], P(None, 'chan', 'tm')
The draws below stay inside these ranges and needn't reach their ends.
Inputs may be any that keep to these rules, and one draw needn't show every extreme that they name: `depth_owner`: the 2 owner groups of one channel differ. In each aligned block of 24 channels no owner group is named by more than 6 channels, and some owner group is named by exactly 6 channels.
All inputs are finite; a program needn't handle non-finite values.
Results may differ from the reference program's by a relative error of at most 0.0003.
Values may be sent and summed in bfloat16 or wider, within the bound.
A program may use at most 64 MiB of HBM per device.

```python
import math
import jax
import jax.numpy as jnp
import numpy as np
from jax import lax

NT = 8192
KLO = 128
NB = 1024
K = 2
CH_DEV = 24
B_OWN = 256
C = 12288
OWNERS = 16
NBIN = 4096
CAP = 6
N_TM = 32
N_CHAN = 16


def draw_depth_slot(key, part):
    key_perm = jax.random.fold_in(key, 11)
    key_pick = jax.random.fold_in(key, 12)
    used_count = B_OWN - max(1, B_OWN // 8)
    middle = (jax.random.permutation(key_perm, B_OWN - 2) + 1).astype(jnp.int32)
    ends = jnp.array([0, B_OWN - 1], jnp.int32)
    used = jnp.concatenate([ends, middle[:used_count - 2]])
    pick = jax.random.randint(key_pick, (C, K), 0, used_count)
    slots = used[pick]
    slots = slots.at[0, 0].set(0).at[0, 1].set(B_OWN - 1)
    return slots.astype(jnp.int32)


def set_ends(values, own_key, low, largest):
    place = [jax.random.randint(jax.random.fold_in(own_key, axis), (), 0, length) for axis, length in enumerate(values.shape)]
    longest = values.shape.index(max(values.shape))
    next_to = place[:longest] + [(place[longest] + 1) % values.shape[longest]] + place[longest + 1:]
    return values.at[tuple(place)].set(low).at[tuple(next_to)].set(largest)


def shard_levels(stream_key, shape, pieces, smallest, high):
    gain = 1.0
    for position, shards_of in pieces:
        draws = jax.random.uniform(jax.random.fold_in(jax.random.fold_in(stream_key, 6), position), (shards_of,), jnp.float32, smallest / len(pieces), high / len(pieces))
        gain = gain * jnp.repeat(jnp.exp(draws), shape[position] // shards_of).reshape((-1,) + (1,) * (len(shape) - 1 - position))
    return gain


def shared_out(own_key, own, number, rows, count, top, reach, skew):
    order = jax.random.permutation(own_key, count)
    heavy_load, common = load_shares(count, rows * top, reach, skew, True), load_shares(count, rows * top, reach, skew, False)
    places = jnp.arange(count)

    def named(lengths, offset_by):
        used = int((lengths > 0).sum())
        fixed = max(1, used // 4)
        moved = fixed + (places - fixed + offset_by * (used - fixed)) % max(1, count - fixed)
        return jnp.zeros((count,), jnp.int32).at[order[jnp.where(places < fixed, places, moved)]].set(jnp.asarray(lengths, jnp.int32))

    lengths = jnp.where(number % 4 == 0, named(heavy_load, number // 4), named(common, number - number // 4 - 1))
    mixed = jax.random.permutation(jax.random.fold_in(own, 3), count)
    source_of, taker = mixed[0:count // 2 * 2:2], mixed[1:count // 2 * 2:2]
    margin = jnp.minimum(lengths[source_of] - 1, reach - lengths[taker]) // 2
    margin = jnp.where((source_of == order[0]) | (taker == order[0]) | (lengths[taker] == 0), 0, jnp.maximum(margin, 0))
    moved = jax.random.randint(jax.random.fold_in(own, 4), (count // 2,), 0, 1 << 20) % (margin + 1)
    lengths = lengths.at[source_of].add(-moved).at[taker].add(moved)
    labels = jnp.searchsorted(jnp.cumsum(lengths), jnp.arange(rows * top), side="right").astype(jnp.int32)
    grid = labels.reshape(top, rows).T
    grid = grid[jax.random.permutation(jax.random.fold_in(own, 1), rows)]
    offset_by = jax.random.randint(jax.random.fold_in(own, 2), (rows, 1), 0, top)
    return jnp.take_along_axis(grid, (jnp.arange(top)[None, :] + offset_by) % top, axis=1)


def load_shares(count, total, most, skew, full):
    weights = [(1 << 20) // math.isqrt(rank ** skew) + 1 for rank in range(1, count + 1)]
    largest = most if full else min(most, max(-(-total // count), total * weights[0] // sum(weights)))
    least = 1 if total - largest >= count - 1 else 0
    counts, surplus = [largest] + [least] * (count - 1), total - largest - least * (count - 1)
    while surplus > 0:
        free = [i for i in range(1, count) if counts[i] < largest] or [i for i in range(1, count) if counts[i] < most]
        mass, remaining = sum([weights[i] for i in free]), surplus
        for i in free:
            more = min(most - counts[i], max(1, remaining * weights[i] // mass), surplus)
            counts[i] = counts[i] + more
            surplus = surplus - more
    return np.array(counts)


def gaussian(stream_key, dims, scale, reach, shards=(), held_as=jnp.bfloat16):
    level = shard_levels(stream_key, dims, shards, -0.22, 0.18) if shards else 1.0
    result = jax.random.normal(stream_key, dims, jnp.float32) * scale * level
    return jnp.minimum(jnp.maximum(result, -reach), reach).astype(held_as)


def setup_inputs(seed: int = 0) -> dict:
    key_of = jax.random.split(jax.random.key(seed), 6)
    raw = gaussian(key_of[0], (NT, C), 1.0, 6.0, ((0, 32), (1, 16)))
    taper = jnp.clip(jnp.exp(jax.random.uniform(key_of[1], (NB,), jnp.float32, math.log(0.1), math.log(1.0))), 0.1, 1.0)
    depth_owner_keys = jax.random.split(jax.random.fold_in(key_of[2], 1), C // CH_DEV)
    depth_owner_turns = jax.random.permutation(jax.random.fold_in(key_of[2], 3), C // CH_DEV)
    depth_owner = jax.vmap(lambda own, number: shared_out(jax.random.fold_in(key_of[2], 2), own, number, CH_DEV, OWNERS, K, CAP, 2))(depth_owner_keys, depth_owner_turns).reshape((C, K))
    depth_slot = draw_depth_slot(jax.random.fold_in(key_of[5], 71), 0)
    intersection = set_ends(jax.random.randint(key_of[4], (C, K), 1, 101), jax.random.fold_in(key_of[4], 1), 1, 100).astype(jnp.int32)
    return dict(raw=raw, taper=taper, depth_owner=depth_owner, depth_slot=depth_slot, intersection=intersection)


def reference(raw, taper, depth_owner, depth_slot, intersection):
    group_cols = CH_DEV * N_TM
    grouped = raw.reshape(NT, N_CHAN, group_cols).transpose(1, 0, 2)
    band_scale = taper * (1.0 / math.sqrt(NT))

    def transform_group(channel_block):
        samples_in = channel_block.astype(jnp.float32)
        full_spec = jnp.fft.rfft(samples_in, axis=0)[KLO:KLO + NB]
        real_part = jnp.real(full_spec) * band_scale[:, None]
        imag_part = jnp.imag(full_spec) * band_scale[:, None]
        return jnp.stack([real_part, imag_part], 0)
    spectra = lax.map(transform_group, grouped)
    spectra = spectra.transpose(0, 3, 1, 2).reshape(C, 2 * NB)
    depth_bin = (depth_owner * B_OWN + depth_slot).astype(jnp.int32)
    weights = intersection.astype(jnp.float32)
    stack_sum = jnp.zeros((NBIN, 2 * NB), jnp.float32)
    weight_sum = jnp.zeros((NBIN,), jnp.float32)
    for which in range(K):
        entry = spectra * weights[:, which][:, None]
        stack_sum = stack_sum + jax.ops.segment_sum(entry, depth_bin[:, which], num_segments=NBIN)
        weight_sum = weight_sum + jax.ops.segment_sum(weights[:, which], depth_bin[:, which], num_segments=NBIN)
    stacked = stack_sum / jnp.maximum(weight_sum, 1.0)[:, None]
    return stacked.reshape(NBIN, 2, NB).transpose(1, 0, 2)
```

```python
import math

import jax
import jax.numpy as jnp
import numpy as np
from jax import lax
from jax.experimental import pallas as pl
from jax.experimental.pallas import tpu as pltpu
from jax.sharding import PartitionSpec as P

NT = 8192
KLO = 128
NB = 1024
B_OWN = 256
N_TM = 32
N_CHAN = 16
CH = 768
TB = 256
TC = 64
NX = 4
BF = jnp.bfloat16
F32 = jnp.float32
MESH = pl.DeviceIdType.MESH


def split_np(a):
    hi = a.astype(jnp.bfloat16)
    lo = (a - hi.astype(np.float64)).astype(jnp.bfloat16)
    return hi, lo


def tables():
    p = np.arange(32)
    s = np.arange(TB)
    ang = 2.0 * np.pi * (np.outer(p, p) % 32) / 32
    first = np.concatenate([np.cos(ang), -np.sin(ang)], 0)
    hi, lo = split_np(first)
    first = np.concatenate([hi, hi, lo], 1)
    mid = 2.0 * np.pi * np.outer(p, s) / NT
    twiddle = np.stack([np.cos(mid), np.sin(mid)]).astype(np.float32)
    q = KLO // 32 + np.arange(NB // 32)
    ang = 2.0 * np.pi * (np.outer(q, s) % TB) / TB
    c, z = np.cos(ang), np.sin(ang)
    second = np.concatenate([np.concatenate([c, z], 1), np.concatenate([-z, c], 1)], 0)
    hi, lo = split_np(second)
    second = np.concatenate([hi, hi, lo], 1)
    return first, twiddle, second


def split(a):
    hi = a.astype(BF)
    lo = (a - hi.astype(F32)).astype(BF)
    return hi, lo


def kernel(
    raw, code, first, twiddle, second, taper, out,
    blocks, codes, acc, packed, parts, rows, samples, mid, outgo, arrived,
    send_raw, recv_raw, send_code, recv_code, fsend_raw, frecv_raw, fsend_code, frecv_code,
    send_x, recv_x, send_t, recv_t, send_f, recv_f, own_sem,
):
    me = lax.axis_index("tm")
    g = lax.axis_index("chan")
    core, x, zl = lax.rem(g, 2), lax.rem(g // 2, NX), g // 8

    def place(dz, dx):
        return (lax.rem(zl + dz, 2) * NX + lax.rem(x + dx, NX)) * 2 + core

    steps = [(0, 0), (1, 0), (0, 1), (1, 1), (0, 3), (1, 3), (0, 2), (1, 2)]
    partner = g + 1 - 2 * core

    barrier = pltpu.get_barrier_semaphore()
    for dz, dx in steps[1:]:
        pl.semaphore_signal(barrier, inc=1, device_id=(me, place(dz, dx)), device_id_type=MESH)
    pl.semaphore_signal(barrier, inc=1, device_id=(me, partner), device_id_type=MESH)

    def greet(d, _):
        pl.semaphore_signal(barrier, inc=1, device_id=(lax.rem(me + d, N_TM), g), device_id_type=MESH)
        return 0

    lax.fori_loop(1, N_TM, greet, 0)
    own_raw = pltpu.make_async_copy(raw.at[pl.ds(pl.multiple_of(x * TC, TC), TC), :], blocks.at[g], own_sem.at[0])
    own_code = pltpu.make_async_copy(code, codes.at[g], own_sem.at[1])
    own_raw.start()
    own_code.start()
    pl.semaphore_wait(barrier, 8 + N_TM - 1)

    def raw_copy(k, dz, dx):
        chunk = pl.ds(pl.multiple_of(lax.rem(x + dx, NX) * TC, TC), TC)
        return pltpu.make_async_remote_copy(
            src_ref=raw.at[chunk, :], dst_ref=blocks.at[g],
            send_sem=send_raw.at[k], recv_sem=recv_raw.at[k],
            device_id=(me, place(dz, dx)), device_id_type=MESH,
        )

    def code_copy(k, dz, dx):
        return pltpu.make_async_remote_copy(
            src_ref=code, dst_ref=codes.at[g],
            send_sem=send_code.at[k], recv_sem=recv_code.at[k],
            device_id=(me, place(dz, dx)), device_id_type=MESH,
        )

    for k, (dz, dx) in enumerate(steps):
        if k:
            code_copy(k, dz, dx).start()
            raw_copy(k, dz, dx).start()

    def forward(k, src):
        return (
            pltpu.make_async_remote_copy(
                src_ref=codes.at[src], dst_ref=codes.at[src],
                send_sem=fsend_code.at[k], recv_sem=frecv_code.at[k],
                device_id=(me, partner), device_id_type=MESH,
            ),
            pltpu.make_async_remote_copy(
                src_ref=blocks.at[src], dst_ref=blocks.at[src],
                send_sem=fsend_raw.at[k], recv_sem=frecv_raw.at[k],
                device_id=(me, partner), device_id_type=MESH,
            ),
        )

    slot_of_row = lax.broadcasted_iota(jnp.int32, (B_OWN, 128), 0).astype(F32).astype(BF)
    ones = jnp.ones((TC, 256), BF)
    acc[...] = jnp.zeros_like(acc)

    def weights_of(src, owner, m):
        c0 = codes[src, pl.ds(m, 1), :]
        c1 = codes[src, pl.ds(6 + m, 1), :]
        c = jnp.where((c0 >> 15) == owner, c0, jnp.where((c1 >> 15) == owner, c1, -1))
        slot = jnp.where(c < 0, -1, (c >> 7) & 255).astype(F32)
        weight = (c & 127).astype(F32)
        slot = jnp.broadcast_to(slot, (16, 128)).astype(BF)
        weight = jnp.broadcast_to(weight, (16, 128)).astype(BF)
        slot = jnp.concatenate([slot] * (B_OWN // 16), 0)
        weight = jnp.concatenate([weight] * (B_OWN // 16), 0)
        return jnp.where(slot_of_row == slot, weight, BF(0))

    def process(src):
        data = [
            jnp.concatenate([blocks[src, :, pl.ds(256 * mm, 256)], ones], 0)
            for mm in range(CH // 256)
        ]
        for xo in range(NX):
            owner = (zl * NX + xo) * 2 + core
            total = None
            for mm in range(CH // 256):
                sel = jnp.concatenate(
                    [weights_of(src, owner, 2 * mm), weights_of(src, owner, 2 * mm + 1)], 1
                )
                part = lax.dot_general(
                    sel, data[mm], (((1,), (1,)), ((), ())), preferred_element_type=F32
                )
                total = part if total is None else total + part
            acc[pl.ds(B_OWN * xo, B_OWN), :] += total

    own_raw.wait()
    own_code.wait()
    for copy in forward(0, g):
        copy.start()
    process(g)
    for copy in forward(0, g + 1 - 2 * core):
        copy.wait_recv()
    process(partner)

    def step(k, _):
        dz = lax.rem(k, 2)
        dx = k // 2
        dx = dx + jnp.where(dx == 2, 1, jnp.where(dx == 3, -1, 0))
        src = (lax.rem(zl + 2 - dz, 2) * NX + lax.rem(x + NX - dx, NX)) * 2 + core
        code_copy(k, dz, dx).wait_recv()
        raw_copy(k, dz, dx).wait_recv()
        for copy in forward(k, src):
            copy.start()
        process(src)
        other = src + 1 - 2 * core
        for copy in forward(k, other):
            copy.wait_recv()
        process(other)
        return 0

    lax.fori_loop(1, 8, step, 0)

    left = lax.broadcasted_iota(jnp.int32, (128, 128), 1) < TC

    def x_copy(dx):
        xo = lax.rem(x + dx, NX)
        return pltpu.make_async_remote_copy(
            src_ref=packed.at[xo], dst_ref=parts.at[x],
            send_sem=send_x.at[dx], recv_sem=recv_x.at[dx],
            device_id=(me, place(0, dx)), device_id_type=MESH,
        )

    def means(r):
        a = acc[pl.ds(r, 128), :]
        return a / jnp.maximum(pltpu.roll(a, TC, 1), 1.0)

    for xo in range(NX):
        low = means(B_OWN * xo)
        high = means(B_OWN * xo + 128)
        packed[xo] = jnp.where(left, low, pltpu.roll(high, TC, 1))
    for dx in (2, 1, 3):
        x_copy(dx).start()
    parts[x] = packed[x]
    for dx in (1, 3, 2):
        x_copy(dx).wait_recv()
    for h in range(2):
        a, b = parts[2 * h], parts[2 * h + 1]
        low = jnp.where(left, a, pltpu.roll(b, TC, 1)).reshape(16, 8, 128)
        high = jnp.where(left, pltpu.roll(a, TC, 1), b).reshape(16, 8, 128)
        rows[pl.ds(0, 16), pl.ds(8 * h, 8), :] = low
        rows[pl.ds(16, 16), pl.ds(8 * h, 8), :] = high

    def eight(i):
        return pl.ds(pl.multiple_of(i * 8, 8), 8)

    def sixteen(i):
        return pl.ds(pl.multiple_of(i * 16, 16), 16)

    def send_rows(d, _):
        to = lax.rem(me + d, N_TM)
        pltpu.make_async_remote_copy(
            src_ref=rows.at[to], dst_ref=samples.at[sixteen(me), :],
            send_sem=send_t, recv_sem=recv_t, device_id=(to, g), device_id_type=MESH,
        ).start()
        return 0

    lax.fori_loop(1, N_TM, send_rows, 0)
    samples[sixteen(me), :] = rows[me]
    all_t = pltpu.make_async_remote_copy(
        src_ref=samples.at[pl.ds(0, 16 * (N_TM - 1)), :],
        dst_ref=samples.at[pl.ds(0, 16 * (N_TM - 1)), :],
        send_sem=send_t, recv_sem=recv_t, device_id=(me, partner), device_id_type=MESH,
    )
    all_t.wait_recv()

    cos, sin = twiddle[0], twiddle[1]
    for b in range(8):
        hi, lo = split(
            jnp.concatenate([samples[pl.ds(b, N_TM, 16), :], samples[pl.ds(8 + b, N_TM, 16), :]], 1)
        )
        y = jnp.dot(first[...], jnp.concatenate([hi, lo, hi], 0), preferred_element_type=F32)
        re, im = y[:32], y[32:]
        z = jnp.concatenate([re * cos + im * sin, im * cos - re * sin], 1)
        hi, lo = split(z)
        mid[pl.ds(32 * b, 32), pl.ds(0, 512)] = hi
        mid[pl.ds(32 * b, 32), pl.ds(512, 512)] = lo
        mid[pl.ds(32 * b, 32), pl.ds(1024, 512)] = hi
    spec = lax.dot_general(
        second[...], mid[...], (((1,), (1,)), ((), ())), preferred_element_type=F32
    )
    outgo[...] = jnp.zeros_like(outgo)
    for r in range(2):
        band = spec[32 * r : 32 * r + 32] * taper[...]
        for h in range(2):
            outgo[pl.ds(2 * r + h, 32, 8), :] = band[:, 128 * h : 128 * h + 128]

    def send_band(d, _):
        to = lax.rem(me + d, N_TM)
        pltpu.make_async_remote_copy(
            src_ref=outgo.at[eight(to), :], dst_ref=arrived.at[eight(me), :],
            send_sem=send_f, recv_sem=recv_f, device_id=(to, g), device_id_type=MESH,
        ).start()
        return 0

    lax.fori_loop(1, N_TM, send_band, 0)
    arrived[eight(me), :] = outgo[eight(me), :]
    all_f = pltpu.make_async_remote_copy(
        src_ref=outgo.at[pl.ds(0, 8 * (N_TM - 1)), :], dst_ref=arrived.at[pl.ds(0, 8 * (N_TM - 1)), :],
        send_sem=send_f, recv_sem=recv_f, device_id=(me, partner), device_id_type=MESH,
    )
    all_f.wait_recv()
    out[...] = arrived[...]

    for k, (dz, dx) in enumerate(steps):
        if k:
            code_copy(k, dz, dx).wait_send()
            raw_copy(k, dz, dx).wait_send()
        for copy in forward(k, g):
            copy.wait_send()
    for dx in (1, 3, 2):
        x_copy(dx).wait_send()
    all_t.wait_send()
    all_f.wait_send()


def local(raw, taper, depth_owner, depth_slot, intersection):
    first, twiddle, second = tables()
    code = (depth_owner * B_OWN + depth_slot) * 128 + intersection
    code = jnp.pad(code.T.reshape(12, 128), ((0, 4), (0, 0)))
    scale = jnp.tile((taper * (1.0 / math.sqrt(NT))).reshape(32, 32), (1, 8))
    vmem = pl.BlockSpec(memory_space=pltpu.VMEM)
    dma = pltpu.SemaphoreType.DMA
    got = pl.pallas_call(
        kernel,
        out_shape=jax.ShapeDtypeStruct((8 * N_TM, 128), F32),
        in_specs=[pl.BlockSpec(memory_space=pl.ANY)] + [vmem] * 5,
        out_specs=vmem,
        scratch_shapes=[
            pltpu.VMEM((N_CHAN, TC, CH), BF),
            pltpu.VMEM((N_CHAN, 16, 128), jnp.int32),
            pltpu.VMEM((NX * B_OWN, 128), F32),
            pltpu.VMEM((NX, 128, 128), F32),
            pltpu.VMEM((NX, 128, 128), F32),
            pltpu.VMEM((N_TM, 16, 128), F32),
            pltpu.VMEM((N_TM * 16, 128), F32),
            pltpu.VMEM((B_OWN, 1536), BF),
            pltpu.VMEM((8 * N_TM, 128), F32),
            pltpu.VMEM((8 * N_TM, 128), F32),
        ]
        + [dma((8,))] * 8
        + [dma((4,)), dma((4,)), dma, dma, dma, dma, dma((2,))],
        compiler_params=pltpu.CompilerParams(
            collective_id=0, has_side_effects=True, vmem_limit_bytes=48 * 2**20
        ),
        name="stack_and_transform",
    )(raw, code, jnp.asarray(first), jnp.asarray(twiddle), jnp.asarray(second), scale)
    got = got.reshape(N_TM, 8, 128)[:, :4].reshape(N_TM, 2, 8, 32)
    return got.transpose(1, 0, 2, 3).reshape(2, B_OWN, 32)


def solution(mesh):
    return jax.shard_map(
        local,
        mesh=mesh,
        in_specs=(P("tm", "chan"), P(), P("chan", None), P("chan", None), P("chan", None)),
        out_specs=P(None, "chan", "tm"),
        check_vma=False,
    )
```

```python
import math

import jax
import jax.numpy as jnp
import numpy as np
from jax import lax
from jax.experimental import pallas as pl
from jax.experimental.pallas import tpu as pltpu
from jax.sharding import PartitionSpec as P

NT = 8192
KLO = 128
NB = 1024
N_TM = 32
N_CHAN = 16
NX = 4
CH = 768
TB = 256
TC = 16
BF = jnp.bfloat16
F32 = jnp.float32
MESH = pl.DeviceIdType.MESH


def split_np(a):
    hi = a.astype(jnp.bfloat16)
    lo = (a - hi.astype(np.float64)).astype(jnp.bfloat16)
    return hi, lo


def tables():
    p = np.arange(32)
    s = np.arange(TB)
    ang = 2.0 * np.pi * (np.outer(p, p) % 32) / 32
    first = np.concatenate([np.cos(ang), -np.sin(ang)], 0)
    hi, lo = split_np(first)
    first = np.concatenate([hi, hi, lo], 1)
    first = np.concatenate([first, np.zeros((64, 32), first.dtype)], 1)
    mid = 2.0 * np.pi * np.outer(p, s) / NT
    twiddle = np.concatenate([np.cos(mid), np.sin(mid)]).astype(np.float32)
    q = KLO // 32 + np.arange(NB // 32)
    ang = 2.0 * np.pi * (np.outer(q, s) % TB) / TB
    c, z = np.cos(ang), np.sin(ang)
    second = np.concatenate([np.concatenate([c, z], 1), np.concatenate([-z, c], 1)], 0)
    hi, lo = split_np(second)
    second = np.concatenate([hi, hi, lo], 1)
    return first, twiddle, second


def split(a):
    hi = a.astype(BF)
    lo = (a - hi.astype(F32)).astype(BF)
    return hi, lo


def kernel(
    raw, owner_in, slot_in, weight_in, first_in, twiddle_in, second_in, taper_in, out,
    owner, slot, weight, first, twiddle, second, taper, scale,
    blocks, codes, acc, sums, parts, rows, samples, mid, outgo, arrived,
    send_raw, recv_raw, send_code, recv_code, send_x, recv_x,
    send_t, recv_t, send_f, recv_f, index_sem, table_sem, own_sem,
):
    me = lax.axis_index("tm")
    g = lax.axis_index("chan")
    core, x, zl = lax.rem(g, 2), lax.rem(g // 2, NX), g // 8
    y, zh = lax.rem(me, 8), me // 8

    index_copies = [
        pltpu.make_async_copy(a, b, index_sem.at[k])
        for k, (a, b) in enumerate([(owner_in, owner), (slot_in, slot), (weight_in, weight)])
    ]
    table_copies = [
        pltpu.make_async_copy(a, b, table_sem.at[k])
        for k, (a, b) in enumerate(
            [(taper_in, taper), (first_in, first), (twiddle_in, twiddle), (second_in, second)]
        )
    ]
    for copy in index_copies:
        copy.start()

    def relative(k):
        step = k // 4
        dx = step + jnp.where(step == 2, 1, jnp.where(step == 3, -1, 0))
        return lax.rem(k // 2, 2), dx, lax.rem(k, 2)

    def to_chan(k):
        dz, dx, dc = relative(k)
        return (lax.rem(zl + dz, 2) * NX + lax.rem(x + dx, NX)) * 2 + lax.rem(core + dc, 2)

    def from_chan(k):
        dz, dx, dc = relative(k)
        return (lax.rem(zl + dz, 2) * NX + lax.rem(x + NX - dx, NX)) * 2 + lax.rem(core + dc, 2)

    def to_tm(n):
        far, m = n // 4, lax.rem(n, 4)
        dy = 4 + jnp.where(lax.rem(far, 2) == 1, -((far + 1) // 2), far // 2)
        dz = jnp.where(m == 0, 2, jnp.where(m == 1, 1, jnp.where(m == 2, 3, 0)))
        return lax.rem(zh + dz, 4) * 8 + lax.rem(y + dy, 8)

    barrier = pltpu.get_barrier_semaphore()

    def greet_tm(n, _):
        pl.semaphore_signal(barrier, inc=1, device_id=(to_tm(n), g), device_id_type=MESH)
        return 0

    def greet_chan(k, _):
        pl.semaphore_signal(barrier, inc=1, device_id=(me, to_chan(k)), device_id_type=MESH)
        return 0

    lax.fori_loop(0, N_TM - 1, greet_tm, 0)
    lax.fori_loop(1, N_CHAN, greet_chan, 0)

    def chunk(i):
        return pl.ds(pl.multiple_of(i * TC, TC), TC)

    own_raw = pltpu.make_async_copy(raw.at[chunk(g), :], blocks.at[g], own_sem)
    own_raw.start()
    for copy in table_copies:
        copy.start()
    for copy in index_copies:
        copy.wait()
    code = (owner[...] * 256 + slot[...]) * 128 + weight[...]
    for j in range(2):
        for m in range(CH // 128):
            r = 6 * j + m
            codes[g, r // 4, pl.ds(r % 4, 1), :] = code[j : j + 1, 128 * m : 128 * m + 128]
    acc[...] = jnp.zeros_like(acc)
    pl.semaphore_wait(barrier, N_TM - 1 + N_CHAN - 1)

    def raw_copy(k):
        to = to_chan(k)
        return pltpu.make_async_remote_copy(
            src_ref=raw.at[chunk(to), :], dst_ref=blocks.at[g],
            send_sem=send_raw.at[k], recv_sem=recv_raw.at[k],
            device_id=(me, to), device_id_type=MESH,
        )

    def code_copy(k):
        return pltpu.make_async_remote_copy(
            src_ref=codes.at[g], dst_ref=codes.at[g],
            send_sem=send_code.at[k], recv_sem=recv_code.at[k],
            device_id=(me, to_chan(k)), device_id_type=MESH,
        )

    def send_group(n, _):
        k = N_CHAN - 1 - n
        code_copy(k).start()
        raw_copy(k).start()
        return 0

    lax.fori_loop(0, N_CHAN - 1, send_group, 0)

    row = lax.broadcasted_iota(jnp.int32, (256, 128), 0).astype(F32).astype(BF)

    def process(src):
        total = None
        for m2 in range(CH // 256):
            data = [blocks[src, :, pl.ds(256 * m2 + 128 * n, 128)] for n in range(2)]
            for j in range(2):
                left, right = [], []
                for n in range(2):
                    r = 6 * j + 2 * m2 + n
                    c = codes[src, r // 4, pl.ds(r % 4, 1), :]

                    def spread(v):
                        return jnp.broadcast_to(v.astype(F32), (16, 128)).astype(BF)

                    key, low, w = spread(c >> 11), spread((c >> 7) & 15), spread(c & 127)
                    key = jnp.concatenate([key] * 16, 0)
                    w = jnp.concatenate([w] * 16, 0)
                    left.append(jnp.where(row == key, w, BF(0)))
                    right.append(
                        jnp.concatenate(
                            [jnp.where(low == BF(v), data[n], BF(0)) for v in range(16)], 0
                        )
                    )
                part = lax.dot_general(
                    jnp.concatenate(left, 1), jnp.concatenate(right, 1),
                    (((1,), (1,)), ((), ())), preferred_element_type=F32,
                )
                total = part if total is None else total + part
        acc[...] += total

    own_raw.wait()
    process(g)

    def step(k, _):
        code_copy(k).wait_recv()
        raw_copy(k).wait_recv()
        process(from_chan(k))
        return 0

    lax.fori_loop(1, N_CHAN, step, 0)
    for h in range(2):
        sums[:, pl.ds(16 * h, 16), :] = acc[:, pl.ds(128 * h, 128)].reshape(16, 16, 128)

    def part(i):
        return pl.ds(pl.multiple_of(i * 32, 32), 32)

    def x_copy(k):
        to = to_chan(k)
        return pltpu.make_async_remote_copy(
            src_ref=sums.at[to], dst_ref=parts.at[part(g), :],
            send_sem=send_x.at[k], recv_sem=recv_x.at[k],
            device_id=(me, to), device_id_type=MESH,
        )

    def send_part(n, _):
        x_copy(N_CHAN - 1 - n).start()
        return 0

    def wait_part(k, _):
        x_copy(k).wait_recv()
        return 0

    lax.fori_loop(0, N_CHAN - 1, send_part, 0)
    parts[part(g), :] = sums[g]
    for copy in table_copies:
        copy.wait()
    quarter = lax.broadcasted_iota(jnp.int32, (8, 128), 1) // 32
    t = taper[...] * (1.0 / math.sqrt(NT))
    for j in range(4):
        line = jnp.zeros((8, 128), F32)
        for n in range(4):
            moved = pltpu.roll(t, (32 * (n - j)) % 128, 1) if n != j else t
            line = jnp.where(quarter == n, moved, line)
        scale[pl.ds(j, 8, 4), :] = line
    every = codes[...].reshape(N_CHAN * 3, 4, 128)
    inverse = []
    for b in range(8):
        hit = jnp.where((every >> 7) == g * 256 + me * 8 + b, every & 127, 0)
        total = jnp.sum(hit, axis=0).astype(F32)
        total = jnp.sum(jnp.sum(total, axis=0, keepdims=True), axis=1, keepdims=True)
        inverse.append(1.0 / jnp.maximum(total, 1.0))
    lax.fori_loop(1, N_CHAN, wait_part, 0)
    for i in range(N_TM):
        rows[i] = parts[pl.ds((i % 2) * 16 + i // 2, 16, 32), :]

    def send_rows(n, _):
        to = to_tm(n)
        pltpu.make_async_remote_copy(
            src_ref=rows.at[to], dst_ref=samples.at[chunk(me), :],
            send_sem=send_t, recv_sem=recv_t, device_id=(to, g), device_id_type=MESH,
        ).start()
        return 0

    lax.fori_loop(0, N_TM - 1, send_rows, 0)
    samples[chunk(me), :] = rows[me]
    all_t = pltpu.make_async_remote_copy(
        src_ref=samples.at[pl.ds(0, 16 * (N_TM - 1)), :],
        dst_ref=samples.at[pl.ds(0, 16 * (N_TM - 1)), :],
        send_sem=send_t, recv_sem=recv_t, device_id=(to_tm(0), g), device_id_type=MESH,
    )
    all_t.wait_recv()

    lane = lax.broadcasted_iota(jnp.int32, (N_TM, 128), 1) // 16
    halves = []
    for u in range(2):
        v = [samples[pl.ds(8 * u + n, N_TM, 16), :] for n in range(8)]
        for bit in (1, 2, 4):
            low = (lane & bit) == 0
            w = list(v)
            for n in range(8):
                if n & bit == 0:
                    w[n] = jnp.where(low, v[n], pltpu.roll(v[n + bit], 16 * bit, 1))
                    w[n + bit] = jnp.where(low, pltpu.roll(v[n], 128 - 16 * bit, 1), v[n + bit])
            v = w
        halves.append(v)
    cos, sin = twiddle[pl.ds(0, 32), :], twiddle[pl.ds(32, 32), :]
    for b in range(8):
        hi, lo = split(jnp.concatenate([halves[0][b], halves[1][b]], 1) * inverse[b])
        here = jnp.concatenate([hi, lo, hi, jnp.zeros_like(hi)], 0)
        f = jnp.dot(first[...], here, preferred_element_type=F32)
        re, im = f[:32], f[32:]
        z = jnp.concatenate([re * cos + im * sin, im * cos - re * sin], 1)
        hi, lo = split(z)
        mid[pl.ds(32 * b, 32), pl.ds(0, 512)] = hi
        mid[pl.ds(32 * b, 32), pl.ds(512, 512)] = lo
        mid[pl.ds(32 * b, 32), pl.ds(1024, 512)] = hi
    spec = lax.dot_general(
        second[...], mid[...], (((1,), (1,)), ((), ())), preferred_element_type=F32
    )
    for r in range(2):
        for h in range(2):
            band = spec[32 * r : 32 * r + 32, 128 * h : 128 * h + 128] * scale[...]
            outgo[:, 2 * r + h, :] = band

    def send_band(n, _):
        to = to_tm(n)
        pltpu.make_async_remote_copy(
            src_ref=outgo.at[to], dst_ref=arrived.at[me],
            send_sem=send_f, recv_sem=recv_f, device_id=(to, g), device_id_type=MESH,
        ).start()
        return 0

    lax.fori_loop(0, N_TM - 1, send_band, 0)
    arrived[me] = outgo[me]
    all_f = pltpu.make_async_remote_copy(
        src_ref=arrived.at[pl.ds(0, N_TM - 1)], dst_ref=arrived.at[pl.ds(0, N_TM - 1)],
        send_sem=send_f, recv_sem=recv_f, device_id=(to_tm(0), g), device_id_type=MESH,
    )
    all_f.wait_recv()
    out[...] = arrived[...]

    def drain(k, _):
        code_copy(k).wait_send()
        raw_copy(k).wait_send()
        x_copy(k).wait_send()
        return 0

    lax.fori_loop(1, N_CHAN, drain, 0)
    all_t.wait_send()
    all_f.wait_send()


def local(raw, taper, depth_owner, depth_slot, intersection):
    first, twiddle, second = tables()
    anywhere = pl.BlockSpec(memory_space=pl.ANY)
    dma = pltpu.SemaphoreType.DMA
    vmem = pltpu.VMEM
    got = pl.pallas_call(
        kernel,
        out_shape=jax.ShapeDtypeStruct((N_TM, 4, 128), F32),
        in_specs=[anywhere] * 8,
        out_specs=pl.BlockSpec(memory_space=pltpu.VMEM),
        scratch_shapes=[
            vmem((2, CH), jnp.int32),
            vmem((2, CH), jnp.int32),
            vmem((2, CH), jnp.int32),
            vmem((64, 128), BF),
            vmem((64, TB), F32),
            vmem((64, 1536), BF),
            vmem((8, 128), F32),
            vmem((32, 128), F32),
            vmem((N_CHAN, TC, CH), BF),
            vmem((N_CHAN, 3, 4, 128), jnp.int32),
            vmem((256, 256), F32),
            vmem((N_CHAN, 32, 128), F32),
            vmem((N_CHAN * 32, 128), F32),
            vmem((N_TM, 16, 128), F32),
            vmem((N_TM * 16, 128), F32),
            vmem((256, 1536), BF),
            vmem((N_TM, 4, 128), F32),
            vmem((N_TM, 4, 128), F32),
        ]
        + [dma((N_CHAN,))] * 6
        + [dma, dma, dma, dma, dma((3,)), dma((4,)), dma],
        compiler_params=pltpu.CompilerParams(
            collective_id=0, has_side_effects=True, vmem_limit_bytes=60 * 2**20
        ),
        name="stack_and_transform",
    )(
        raw, depth_owner.T, depth_slot.T, intersection.T,
        jnp.asarray(first), jnp.asarray(twiddle), jnp.asarray(second), taper.reshape(8, 128),
    )
    got = got.reshape(N_TM, 2, 8, 32)
    return got.transpose(1, 0, 2, 3).reshape(2, 256, 32)


def solution(mesh):
    return jax.shard_map(
        local,
        mesh=mesh,
        in_specs=(P("tm", "chan"), P(), P("chan", None), P("chan", None), P("chan", None)),
        out_specs=P(None, "chan", "tm"),
        check_vma=False,
    )
```

```python
import math

import jax
import jax.numpy as jnp
import numpy as np
from jax import lax
from jax.experimental import pallas as pl
from jax.experimental.pallas import tpu as pltpu
from jax.sharding import PartitionSpec as P

NT = 8192
KLO = 128
NB = 1024
N_TM = 32
N_CHAN = 16
NX = 4
CH = 768
TB = 256
TC = 16
BF = jnp.bfloat16
F32 = jnp.float32
MESH = pl.DeviceIdType.MESH


def split_np(a):
    hi = a.astype(jnp.bfloat16)
    lo = (a - hi.astype(np.float64)).astype(jnp.bfloat16)
    return hi, lo


def tables():
    p = np.arange(32)
    s = np.arange(TB)
    ang = 2.0 * np.pi * (np.outer(p, p) % 32) / 32
    first = np.concatenate([np.cos(ang), -np.sin(ang)], 0)
    hi, lo = split_np(first)
    first = np.concatenate([hi, hi, lo], 1)
    first = np.concatenate([first, np.zeros((64, 32), first.dtype)], 1)
    mid = 2.0 * np.pi * np.outer(p, s) / NT
    twiddle = np.concatenate([np.cos(mid), np.sin(mid)]).astype(np.float32)
    q = KLO // 32 + np.arange(NB // 32)
    ang = 2.0 * np.pi * (np.outer(q, s) % TB) / TB
    c, z = np.cos(ang), np.sin(ang)
    second = np.concatenate([np.concatenate([c, z], 1), np.concatenate([-z, c], 1)], 0)
    hi, lo = split_np(second)
    second = np.concatenate([hi, hi, lo], 1)
    return first, twiddle, second


def split(a):
    hi = a.astype(BF)
    lo = (a - hi.astype(F32)).astype(BF)
    return hi, lo


def kernel(
    raw, owner_in, slot_in, weight_in, first_in, twiddle_in, second_in, taper_in, out,
    owner, slot, weight, first, twiddle, second, taper, scale,
    blocks, codes, acc, sums, parts, rows, samples, mid, outgo, arrived,
    send_raw, recv_raw, send_code, recv_code, send_x, recv_x,
    send_t, recv_t, send_f, recv_f, index_sem, table_sem, own_sem, ring_sem,
):
    me = lax.axis_index("tm")
    g = lax.axis_index("chan")
    core, x, zl = lax.rem(g, 2), lax.rem(g // 2, NX), g // 8
    y, zh = lax.rem(me, 8), me // 8

    index_copies = [
        pltpu.make_async_copy(a, b, index_sem.at[k])
        for k, (a, b) in enumerate([(owner_in, owner), (slot_in, slot), (weight_in, weight)])
    ]
    table_copies = [
        pltpu.make_async_copy(a, b, table_sem.at[k])
        for k, (a, b) in enumerate(
            [(taper_in, taper), (first_in, first), (twiddle_in, twiddle), (second_in, second)]
        )
    ]
    for copy in index_copies:
        copy.start()

    def relative(k):
        step = k // 4
        dx = step + jnp.where(step == 2, 1, jnp.where(step == 3, -1, 0))
        return lax.rem(k // 2, 2), dx, lax.rem(k, 2)

    def to_chan(k):
        dz, dx, dc = relative(k)
        return (lax.rem(zl + dz, 2) * NX + lax.rem(x + dx, NX)) * 2 + lax.rem(core + dc, 2)

    def from_chan(k):
        dz, dx, dc = relative(k)
        return (lax.rem(zl + dz, 2) * NX + lax.rem(x + NX - dx, NX)) * 2 + lax.rem(core + dc, 2)

    def to_tm(n):
        far, m = n // 4, lax.rem(n, 4)
        dy = 4 + jnp.where(lax.rem(far, 2) == 1, -((far + 1) // 2), far // 2)
        dz = jnp.where(m == 0, 2, jnp.where(m == 1, 1, jnp.where(m == 2, 3, 0)))
        return lax.rem(zh + dz, 4) * 8 + lax.rem(y + dy, 8)

    barrier = pltpu.get_barrier_semaphore()

    def along_y(d):
        return zh * 8 + lax.rem(y + d, 8)

    def greet_y(d, _):
        pl.semaphore_signal(barrier, inc=1, device_id=(along_y(d), g), device_id_type=MESH)
        return 0

    def greet_z(d, _):
        to = lax.rem(zh + d, 4) * 8 + y
        pl.semaphore_signal(barrier, inc=1, device_id=(to, g), device_id_type=MESH)
        return 0

    def tell_y(d, _):
        pl.semaphore_signal(ring_sem, inc=1, device_id=(along_y(d), g), device_id_type=MESH)
        return 0

    def greet_chan(k, _):
        pl.semaphore_signal(barrier, inc=1, device_id=(me, to_chan(k)), device_id_type=MESH)
        return 0

    lax.fori_loop(1, 8, greet_y, 0)
    lax.fori_loop(1, 4, greet_z, 0)
    lax.fori_loop(1, N_CHAN, greet_chan, 0)

    def chunk(i):
        return pl.ds(pl.multiple_of(i * TC, TC), TC)

    own_raw = pltpu.make_async_copy(raw.at[chunk(g), :], blocks.at[g], own_sem)
    own_raw.start()
    for copy in table_copies:
        copy.start()
    for copy in index_copies:
        copy.wait()
    code = (owner[...] * 256 + slot[...]) * 128 + weight[...]
    for j in range(2):
        for m in range(CH // 128):
            r = 6 * j + m
            codes[g, r // 4, pl.ds(r % 4, 1), :] = code[j : j + 1, 128 * m : 128 * m + 128]
    acc[...] = jnp.zeros_like(acc)
    pl.semaphore_wait(barrier, 7 + 3 + N_CHAN - 1)

    def raw_copy(k):
        to = to_chan(k)
        return pltpu.make_async_remote_copy(
            src_ref=raw.at[chunk(to), :], dst_ref=blocks.at[g],
            send_sem=send_raw.at[k], recv_sem=recv_raw.at[k],
            device_id=(me, to), device_id_type=MESH,
        )

    def code_copy(k):
        return pltpu.make_async_remote_copy(
            src_ref=codes.at[g], dst_ref=codes.at[g],
            send_sem=send_code.at[k], recv_sem=recv_code.at[k],
            device_id=(me, to_chan(k)), device_id_type=MESH,
        )

    def send_group(n, _):
        k = n + 1
        code_copy(k).start()
        raw_copy(k).start()
        return 0

    lax.fori_loop(0, N_CHAN - 1, send_group, 0)
    lax.fori_loop(1, 8, tell_y, 0)

    row = lax.broadcasted_iota(jnp.int32, (256, 128), 0).astype(F32).astype(BF)

    def process(src):
        total = None
        for m2 in range(CH // 256):
            data = [blocks[src, :, pl.ds(256 * m2 + 128 * n, 128)] for n in range(2)]
            for j in range(2):
                left, right = [], []
                for n in range(2):
                    r = 6 * j + 2 * m2 + n
                    c = codes[src, r // 4, pl.ds(r % 4, 1), :]

                    def spread(v):
                        return jnp.broadcast_to(v.astype(F32), (16, 128)).astype(BF)

                    key = spread(((c >> 15) << 4) + ((c >> 7) & 15))
                    low = spread(((c >> 11) & 1) * 8 + ((c >> 12) & 7))
                    w = spread(c & 127)
                    key = jnp.concatenate([key] * 16, 0)
                    w = jnp.concatenate([w] * 16, 0)
                    left.append(jnp.where(row == key, w, BF(0)))
                    right.append(
                        jnp.concatenate(
                            [jnp.where(low == BF(v), data[n], BF(0)) for v in range(16)], 0
                        )
                    )
                part = lax.dot_general(
                    jnp.concatenate(left, 1), jnp.concatenate(right, 1),
                    (((1,), (1,)), ((), ())), preferred_element_type=F32,
                )
                total = part if total is None else total + part
        acc[...] += total

    own_raw.wait()
    process(g)

    def step(k, _):
        code_copy(k).wait_recv()
        raw_copy(k).wait_recv()
        process(from_chan(k))
        return 0

    lax.fori_loop(1, N_CHAN, step, 0)
    for h in range(2):
        sums[:, pl.ds(16 * h, 16), :] = acc[:, pl.ds(128 * h, 128)].reshape(16, 16, 128)

    def part(i):
        return pl.ds(pl.multiple_of(i * 32, 32), 32)

    def x_copy(k):
        to = to_chan(k)
        return pltpu.make_async_remote_copy(
            src_ref=sums.at[to], dst_ref=parts.at[part(g), :],
            send_sem=send_x.at[k], recv_sem=recv_x.at[k],
            device_id=(me, to), device_id_type=MESH,
        )

    def send_part(n, _):
        x_copy(N_CHAN - 1 - n).start()
        return 0

    def wait_part(k, _):
        x_copy(k).wait_recv()
        return 0

    lax.fori_loop(0, N_CHAN - 1, send_part, 0)
    parts[part(g), :] = sums[g]
    for copy in table_copies:
        copy.wait()
    quarter = lax.broadcasted_iota(jnp.int32, (8, 128), 1) // 32
    t = taper[...] * (1.0 / math.sqrt(NT))
    for j in range(4):
        line = jnp.zeros((8, 128), F32)
        for n in range(4):
            moved = pltpu.roll(t, (32 * (n - j)) % 128, 1) if n != j else t
            line = jnp.where(quarter == n, moved, line)
        scale[pl.ds(j, 8, 4), :] = line
    every = codes[...].reshape(N_CHAN * 3, 4, 128)
    inverse = []
    for b in range(8):
        hit = jnp.where((every >> 7) == g * 256 + b * 32 + me, every & 127, 0)
        total = jnp.sum(hit, axis=0).astype(F32)
        total = jnp.sum(jnp.sum(total, axis=0, keepdims=True), axis=1, keepdims=True)
        inverse.append(1.0 / jnp.maximum(total, 1.0))
    lax.fori_loop(1, N_CHAN, wait_part, 0)
    for i in range(N_TM):
        rows[i] = parts[pl.ds(i, 16, 32), :]

    def send_rows(n, _):
        to = to_tm(n)
        pltpu.make_async_remote_copy(
            src_ref=rows.at[to], dst_ref=samples.at[chunk(me), :],
            send_sem=send_t, recv_sem=recv_t, device_id=(to, g), device_id_type=MESH,
        ).start()
        return 0

    pl.semaphore_wait(ring_sem, 7)
    lax.fori_loop(0, N_TM - 1, send_rows, 0)
    samples[chunk(me), :] = rows[me]
    all_t = pltpu.make_async_remote_copy(
        src_ref=samples.at[pl.ds(0, 16 * (N_TM - 1)), :],
        dst_ref=samples.at[pl.ds(0, 16 * (N_TM - 1)), :],
        send_sem=send_t, recv_sem=recv_t, device_id=(to_tm(0), g), device_id_type=MESH,
    )
    all_t.wait_recv()

    lane = lax.broadcasted_iota(jnp.int32, (N_TM, 128), 1) // 16
    halves = []
    for u in range(2):
        v = [samples[pl.ds(8 * u + n, N_TM, 16), :] for n in range(8)]
        for bit in (1, 2, 4):
            low = (lane & bit) == 0
            w = list(v)
            for n in range(8):
                if n & bit == 0:
                    w[n] = jnp.where(low, v[n], pltpu.roll(v[n + bit], 16 * bit, 1))
                    w[n + bit] = jnp.where(low, pltpu.roll(v[n], 128 - 16 * bit, 1), v[n + bit])
            v = w
        halves.append(v)
    cos, sin = twiddle[pl.ds(0, 32), :], twiddle[pl.ds(32, 32), :]
    for b in range(8):
        hi, lo = split(jnp.concatenate([halves[0][b], halves[1][b]], 1) * inverse[b])
        here = jnp.concatenate([hi, lo, hi, jnp.zeros_like(hi)], 0)
        f = jnp.dot(first[...], here, preferred_element_type=F32)
        re, im = f[:32], f[32:]
        z = jnp.concatenate([re * cos + im * sin, im * cos - re * sin], 1)
        hi, lo = split(z)
        mid[pl.ds(32 * b, 32), pl.ds(0, 512)] = hi
        mid[pl.ds(32 * b, 32), pl.ds(512, 512)] = lo
        mid[pl.ds(32 * b, 32), pl.ds(1024, 512)] = hi
    spec = lax.dot_general(
        second[...], mid[...], (((1,), (1,)), ((), ())), preferred_element_type=F32
    )
    for r in range(2):
        for h in range(2):
            band = spec[32 * r : 32 * r + 32, 128 * h : 128 * h + 128] * scale[...]
            outgo[:, 2 * r + h, :] = band

    def send_band(n, _):
        to = to_tm(n)
        pltpu.make_async_remote_copy(
            src_ref=outgo.at[to], dst_ref=arrived.at[me],
            send_sem=send_f, recv_sem=recv_f, device_id=(to, g), device_id_type=MESH,
        ).start()
        return 0

    lax.fori_loop(0, N_TM - 1, send_band, 0)
    arrived[me] = outgo[me]
    all_f = pltpu.make_async_remote_copy(
        src_ref=arrived.at[pl.ds(0, N_TM - 1)], dst_ref=arrived.at[pl.ds(0, N_TM - 1)],
        send_sem=send_f, recv_sem=recv_f, device_id=(to_tm(0), g), device_id_type=MESH,
    )
    all_f.wait_recv()
    for r in range(2):
        for h in range(2):
            turned = arrived[:, 2 * r + h, :].T
            out[r, :, pl.ds(128 * h, 128)] = jnp.concatenate(
                [turned[32 * n : 32 * n + 32] for n in range(4)], 1
            )

    def drain(k, _):
        code_copy(k).wait_send()
        raw_copy(k).wait_send()
        x_copy(k).wait_send()
        return 0

    lax.fori_loop(1, N_CHAN, drain, 0)
    all_t.wait_send()
    all_f.wait_send()


def local(raw, taper, depth_owner, depth_slot, intersection):
    first, twiddle, second = tables()
    anywhere = pl.BlockSpec(memory_space=pl.ANY)
    dma = pltpu.SemaphoreType.DMA
    vmem = pltpu.VMEM
    got = pl.pallas_call(
        kernel,
        out_shape=jax.ShapeDtypeStruct((2, 32, 256), F32),
        in_specs=[anywhere] * 8,
        out_specs=pl.BlockSpec(memory_space=pltpu.VMEM),
        scratch_shapes=[
            vmem((2, CH), jnp.int32),
            vmem((2, CH), jnp.int32),
            vmem((2, CH), jnp.int32),
            vmem((64, 128), BF),
            vmem((64, TB), F32),
            vmem((64, 1536), BF),
            vmem((8, 128), F32),
            vmem((32, 128), F32),
            vmem((N_CHAN, TC, CH), BF),
            vmem((N_CHAN, 3, 4, 128), jnp.int32),
            vmem((256, 256), F32),
            vmem((N_CHAN, 32, 128), F32),
            vmem((N_CHAN * 32, 128), F32),
            vmem((N_TM, 16, 128), F32),
            vmem((N_TM * 16, 128), F32),
            vmem((256, 1536), BF),
            vmem((N_TM, 4, 128), F32),
            vmem((N_TM, 4, 128), F32),
        ]
        + [dma((N_CHAN,))] * 6
        + [dma, dma, dma, dma, dma((3,)), dma((4,)), dma, pltpu.SemaphoreType.REGULAR],
        compiler_params=pltpu.CompilerParams(
            collective_id=0, has_side_effects=True, vmem_limit_bytes=60 * 2**20
        ),
        name="stack_and_transform",
    )(
        raw, depth_owner.T, depth_slot.T, intersection.T,
        jnp.asarray(first), jnp.asarray(twiddle), jnp.asarray(second), taper.reshape(8, 128),
    )
    return got.transpose(0, 2, 1)


def solution(mesh):
    return jax.shard_map(
        local,
        mesh=mesh,
        in_specs=(P("tm", "chan"), P(), P("chan", None), P("chan", None), P("chan", None)),
        out_specs=P(None, "chan", "tm"),
        check_vma=False,
    )
```

```python
import math

import jax
import jax.numpy as jnp
import numpy as np
from jax import lax
from jax.experimental import pallas as pl
from jax.experimental.pallas import tpu as pltpu
from jax.sharding import PartitionSpec as P

NT = 8192
KLO = 128
NB = 1024
N_TM = 32
N_CHAN = 16
NX = 4
CH = 768
TB = 256
TC = 16
BF = jnp.bfloat16
F32 = jnp.float32
MESH = pl.DeviceIdType.MESH


def split_np(a):
    hi = a.astype(jnp.bfloat16)
    lo = (a - hi.astype(np.float64)).astype(jnp.bfloat16)
    return hi, lo


def tables():
    p = np.arange(32)
    s = np.arange(TB)
    ang = 2.0 * np.pi * (np.outer(p, p) % 32) / 32
    first = np.concatenate([np.cos(ang), -np.sin(ang)], 0)
    hi, lo = split_np(first)
    first = np.concatenate([hi, hi, lo], 1)
    first = np.concatenate([first, np.zeros((64, 32), first.dtype)], 1)
    mid = 2.0 * np.pi * np.outer(p, s) / NT
    twiddle = np.concatenate([np.cos(mid), np.sin(mid)]).astype(np.float32)
    q = KLO // 32 + np.arange(NB // 32)
    ang = 2.0 * np.pi * (np.outer(q, s) % TB) / TB
    c, z = np.cos(ang), np.sin(ang)
    second = np.concatenate([np.concatenate([c, z], 1), np.concatenate([-z, c], 1)], 0)
    hi, lo = split_np(second)
    second = np.concatenate([hi, hi, lo], 1)
    return first, twiddle, second


def split(a):
    hi = a.astype(BF)
    lo = (a - hi.astype(F32)).astype(BF)
    return hi, lo


def kernel(
    raw, owner_in, slot_in, weight_in, first_in, twiddle_in, second_in, taper_in, out,
    owner, slot, weight, first, twiddle, second, taper, scale,
    blocks, codes, acc, sums, parts, rows, samples, mid, outgo, arrived,
    send_raw, recv_raw, send_code, recv_code, send_x, recv_x,
    send_t, recv_t, send_f, recv_f, index_sem, table_sem, own_sem, ring_sem,
):
    me = lax.axis_index("tm")
    g = lax.axis_index("chan")
    core, x, zl = lax.rem(g, 2), lax.rem(g // 2, NX), g // 8
    y, zh = lax.rem(me, 8), me // 8

    index_copies = [
        pltpu.make_async_copy(a, b, index_sem.at[k])
        for k, (a, b) in enumerate([(owner_in, owner), (slot_in, slot), (weight_in, weight)])
    ]
    table_copies = [
        pltpu.make_async_copy(a, b, table_sem.at[k])
        for k, (a, b) in enumerate(
            [(taper_in, taper), (first_in, first), (twiddle_in, twiddle), (second_in, second)]
        )
    ]
    for copy in index_copies:
        copy.start()

    def relative(k):
        step = k // 4
        dx = step + jnp.where(step == 2, 1, jnp.where(step == 3, -1, 0))
        return lax.rem(k // 2, 2), dx, lax.rem(k, 2)

    def to_chan(k):
        dz, dx, dc = relative(k)
        return (lax.rem(zl + dz, 2) * NX + lax.rem(x + dx, NX)) * 2 + lax.rem(core + dc, 2)

    def from_chan(k):
        dz, dx, dc = relative(k)
        return (lax.rem(zl + dz, 2) * NX + lax.rem(x + NX - dx, NX)) * 2 + lax.rem(core + dc, 2)

    def place_of(chan):
        dz = lax.rem(chan // 8 + zl, 2)
        dx = lax.rem(x + NX - (chan // 2) % NX, NX)
        near = dx + jnp.where(dx == 2, 1, jnp.where(dx == 3, -1, 0))
        return near * 4 + dz * 2 + lax.rem(chan % 2 + core, 2)

    def to_tm(n):
        far, m = n // 4, lax.rem(n, 4)
        dy = 4 + jnp.where(lax.rem(far, 2) == 1, -((far + 1) // 2), far // 2)
        dz = jnp.where(m == 0, 2, jnp.where(m == 1, 1, jnp.where(m == 2, 3, 0)))
        return lax.rem(zh + dz, 4) * 8 + lax.rem(y + dy, 8)

    barrier = pltpu.get_barrier_semaphore()

    def along_y(d):
        return zh * 8 + lax.rem(y + d, 8)

    def greet_y(d, _):
        pl.semaphore_signal(barrier, inc=1, device_id=(along_y(d), g), device_id_type=MESH)
        return 0

    def greet_z(d, _):
        to = lax.rem(zh + d, 4) * 8 + y
        pl.semaphore_signal(barrier, inc=1, device_id=(to, g), device_id_type=MESH)
        return 0

    def tell_y(d, _):
        pl.semaphore_signal(ring_sem, inc=1, device_id=(along_y(d), g), device_id_type=MESH)
        return 0

    def greet_chan(k, _):
        pl.semaphore_signal(barrier, inc=1, device_id=(me, to_chan(k)), device_id_type=MESH)
        return 0

    lax.fori_loop(1, 8, greet_y, 0)
    lax.fori_loop(1, 4, greet_z, 0)
    lax.fori_loop(1, N_CHAN, greet_chan, 0)

    def chunk(i):
        return pl.ds(pl.multiple_of(i * TC, TC), TC)

    own_raw = pltpu.make_async_copy(raw.at[chunk(g), :], blocks.at[g], own_sem)
    own_raw.start()
    for copy in index_copies:
        copy.wait()
    code = (owner[...] * 256 + slot[...]) * 128 + weight[...]
    for j in range(2):
        for m in range(CH // 128):
            r = 6 * j + m
            codes[g, r // 4, pl.ds(r % 4, 1), :] = code[j : j + 1, 128 * m : 128 * m + 128]
    acc[...] = jnp.zeros_like(acc)
    pl.semaphore_wait(barrier, 7 + 3 + N_CHAN - 1)

    def raw_copy(k):
        to = to_chan(k)
        return pltpu.make_async_remote_copy(
            src_ref=raw.at[chunk(to), :], dst_ref=blocks.at[g],
            send_sem=send_raw.at[k], recv_sem=recv_raw.at[k],
            device_id=(me, to), device_id_type=MESH,
        )

    def code_copy(k):
        return pltpu.make_async_remote_copy(
            src_ref=codes.at[g], dst_ref=codes.at[g],
            send_sem=send_code.at[k], recv_sem=recv_code.at[k],
            device_id=(me, to_chan(k)), device_id_type=MESH,
        )

    def send_group(n, _):
        k = n + 1
        code_copy(k).start()
        raw_copy(k).start()
        return 0

    lax.fori_loop(0, N_CHAN - 1, send_group, 0)
    lax.fori_loop(1, 8, tell_y, 0)
    for copy in table_copies:
        copy.start()

    row = lax.broadcasted_iota(jnp.int32, (256, 128), 0).astype(F32).astype(BF)

    def process(src):
        total = None
        for m2 in range(CH // 256):
            data = [blocks[src, :, pl.ds(256 * m2 + 128 * n, 128)] for n in range(2)]
            for j in range(2):
                left, right = [], []
                for n in range(2):
                    r = 6 * j + 2 * m2 + n
                    c = codes[src, r // 4, pl.ds(r % 4, 1), :]

                    def spread(v):
                        return jnp.broadcast_to(v.astype(F32), (16, 128)).astype(BF)

                    key = spread(((c >> 15) << 4) + ((c >> 7) & 15))
                    low = spread(((c >> 11) & 1) * 8 + ((c >> 12) & 7))
                    w = spread(c & 127)
                    key = jnp.concatenate([key] * 16, 0)
                    w = jnp.concatenate([w] * 16, 0)
                    left.append(jnp.where(row == key, w, BF(0)))
                    right.append(
                        jnp.concatenate(
                            [jnp.where(low == BF(v), data[n], BF(0)) for v in range(16)], 0
                        )
                    )
                part = lax.dot_general(
                    jnp.concatenate(left, 1), jnp.concatenate(right, 1),
                    (((1,), (1,)), ((), ())), preferred_element_type=F32,
                )
                total = part if total is None else total + part
        acc[...] += total

    own_raw.wait()
    process(g)

    def step(k, _):
        code_copy(k).wait_recv()
        raw_copy(k).wait_recv()
        process(from_chan(k))
        return 0

    lax.fori_loop(1, N_CHAN, step, 0)
    for h in range(2):
        sums[:, pl.ds(16 * h, 16), :] = acc[:, pl.ds(128 * h, 128)].reshape(16, 16, 128)

    def part(i):
        return pl.ds(pl.multiple_of(i * 32, 32), 32)

    def x_copy(k):
        to = to_chan(k)
        return pltpu.make_async_remote_copy(
            src_ref=sums.at[to], dst_ref=parts.at[part(k), :],
            send_sem=send_x.at[k], recv_sem=recv_x.at[k],
            device_id=(me, to), device_id_type=MESH,
        )

    def send_part(n, _):
        x_copy(n + 1).start()
        return 0

    def wait_part(k, _):
        x_copy(k).wait_recv()
        return 0

    lax.fori_loop(0, N_CHAN - 1, send_part, 0)
    parts[pl.ds(0, 32), :] = sums[g]
    for copy in table_copies:
        copy.wait()
    quarter = lax.broadcasted_iota(jnp.int32, (8, 128), 1) // 32
    t = taper[...] * (1.0 / math.sqrt(NT))
    for j in range(4):
        line = jnp.zeros((8, 128), F32)
        for n in range(4):
            moved = pltpu.roll(t, (32 * (n - j)) % 128, 1) if n != j else t
            line = jnp.where(quarter == n, moved, line)
        scale[pl.ds(j, 8, 4), :] = line
    every = codes[...].reshape(N_CHAN * 3, 4, 128)
    inverse = []
    for b in range(8):
        hit = jnp.where((every >> 7) == g * 256 + b * 32 + me, every & 127, 0)
        total = jnp.sum(hit, axis=0).astype(F32)
        total = jnp.sum(jnp.sum(total, axis=0, keepdims=True), axis=1, keepdims=True)
        inverse.append(1.0 / jnp.maximum(total, 1.0))

    def send_rows(half):
        def send(n, _):
            to = to_tm(n)
            rows[to, pl.ds(8 * half, 8), :] = parts[pl.ds(256 * half + to, 8, 32), :]
            pltpu.make_async_remote_copy(
                src_ref=rows.at[to, pl.ds(8 * half, 8), :],
                dst_ref=samples.at[pl.ds(pl.multiple_of(me * 16 + 8 * half, 8), 8), :],
                send_sem=send_t, recv_sem=recv_t, device_id=(to, g), device_id_type=MESH,
            ).start()
            return 0

        lax.fori_loop(0, N_TM - 1, send, 0)

    pl.semaphore_wait(ring_sem, 7)
    for half in range(2):
        lax.fori_loop(max(1, 8 * half), 8 * half + 8, wait_part, 0)
        send_rows(half)
    samples[chunk(me), :] = parts[pl.ds(me, 16, 32), :]
    all_t = pltpu.make_async_remote_copy(
        src_ref=samples.at[pl.ds(0, 16 * (N_TM - 1)), :],
        dst_ref=samples.at[pl.ds(0, 16 * (N_TM - 1)), :],
        send_sem=send_t, recv_sem=recv_t, device_id=(to_tm(0), g), device_id_type=MESH,
    )
    all_t.wait_recv()

    lane = lax.broadcasted_iota(jnp.int32, (N_TM, 128), 1) // 16
    halves = []
    for u in range(2):
        v = [samples[pl.ds(place_of(8 * u + n), N_TM, 16), :] for n in range(8)]
        for bit in (1, 2, 4):
            low = (lane & bit) == 0
            w = list(v)
            for n in range(8):
                if n & bit == 0:
                    w[n] = jnp.where(low, v[n], pltpu.roll(v[n + bit], 16 * bit, 1))
                    w[n + bit] = jnp.where(low, pltpu.roll(v[n], 128 - 16 * bit, 1), v[n + bit])
            v = w
        halves.append(v)
    cos, sin = twiddle[pl.ds(0, 32), :], twiddle[pl.ds(32, 32), :]
    for b in range(8):
        hi, lo = split(jnp.concatenate([halves[0][b], halves[1][b]], 1) * inverse[b])
        here = jnp.concatenate([hi, lo, hi, jnp.zeros_like(hi)], 0)
        f = jnp.dot(first[...], here, preferred_element_type=F32)
        re, im = f[:32], f[32:]
        z = jnp.concatenate([re * cos + im * sin, im * cos - re * sin], 1)
        hi, lo = split(z)
        mid[pl.ds(32 * b, 32), pl.ds(0, 512)] = hi
        mid[pl.ds(32 * b, 32), pl.ds(512, 512)] = lo
        mid[pl.ds(32 * b, 32), pl.ds(1024, 512)] = hi
    spec = lax.dot_general(
        second[...], mid[...], (((1,), (1,)), ((), ())), preferred_element_type=F32
    )
    for r in range(2):
        for h in range(2):
            band = spec[32 * r : 32 * r + 32, 128 * h : 128 * h + 128] * scale[...]
            outgo[:, 2 * r + h, :] = band

    def send_band(n, _):
        to = to_tm(n)
        pltpu.make_async_remote_copy(
            src_ref=outgo.at[to], dst_ref=arrived.at[me],
            send_sem=send_f, recv_sem=recv_f, device_id=(to, g), device_id_type=MESH,
        ).start()
        return 0

    lax.fori_loop(0, N_TM - 1, send_band, 0)
    arrived[me] = outgo[me]
    all_f = pltpu.make_async_remote_copy(
        src_ref=arrived.at[pl.ds(0, N_TM - 1)], dst_ref=arrived.at[pl.ds(0, N_TM - 1)],
        send_sem=send_f, recv_sem=recv_f, device_id=(to_tm(0), g), device_id_type=MESH,
    )
    all_f.wait_recv()
    for r in range(2):
        for h in range(2):
            turned = arrived[:, 2 * r + h, :].T
            out[r, :, pl.ds(128 * h, 128)] = jnp.concatenate(
                [turned[32 * n : 32 * n + 32] for n in range(4)], 1
            )

    def drain(k, _):
        code_copy(k).wait_send()
        raw_copy(k).wait_send()
        x_copy(k).wait_send()
        return 0

    lax.fori_loop(1, N_CHAN, drain, 0)
    all_t.wait_send()
    all_f.wait_send()


def local(raw, taper, depth_owner, depth_slot, intersection):
    first, twiddle, second = tables()
    anywhere = pl.BlockSpec(memory_space=pl.ANY)
    dma = pltpu.SemaphoreType.DMA
    vmem = pltpu.VMEM
    got = pl.pallas_call(
        kernel,
        out_shape=jax.ShapeDtypeStruct((2, 32, 256), F32),
        in_specs=[anywhere] * 8,
        out_specs=pl.BlockSpec(memory_space=pltpu.VMEM),
        scratch_shapes=[
            vmem((2, CH), jnp.int32),
            vmem((2, CH), jnp.int32),
            vmem((2, CH), jnp.int32),
            vmem((64, 128), BF),
            vmem((64, TB), F32),
            vmem((64, 1536), BF),
            vmem((8, 128), F32),
            vmem((32, 128), F32),
            vmem((N_CHAN, TC, CH), BF),
            vmem((N_CHAN, 3, 4, 128), jnp.int32),
            vmem((256, 256), F32),
            vmem((N_CHAN, 32, 128), F32),
            vmem((N_CHAN * 32, 128), F32),
            vmem((N_TM, 16, 128), F32),
            vmem((N_TM * 16, 128), F32),
            vmem((256, 1536), BF),
            vmem((N_TM, 4, 128), F32),
            vmem((N_TM, 4, 128), F32),
        ]
        + [dma((N_CHAN,))] * 6
        + [dma, dma, dma, dma, dma((3,)), dma((4,)), dma, pltpu.SemaphoreType.REGULAR],
        compiler_params=pltpu.CompilerParams(
            collective_id=0, has_side_effects=True, vmem_limit_bytes=60 * 2**20
        ),
        name="stack_and_transform",
    )(
        raw, depth_owner.T, depth_slot.T, intersection.T,
        jnp.asarray(first), jnp.asarray(twiddle), jnp.asarray(second), taper.reshape(8, 128),
    )
    return got.transpose(0, 2, 1)


def solution(mesh):
    return jax.shard_map(
        local,
        mesh=mesh,
        in_specs=(P("tm", "chan"), P(), P("chan", None), P("chan", None), P("chan", None)),
        out_specs=P(None, "chan", "tm"),
        check_vma=False,
    )
```

```python
import math

import jax
import jax.numpy as jnp
import numpy as np
from jax import lax
from jax.experimental import pallas as pl
from jax.experimental.pallas import tpu as pltpu
from jax.sharding import PartitionSpec as P

NT = 8192
KLO = 128
NB = 1024
N_TM = 32
N_CHAN = 16
NX = 4
CH = 768
TB = 256
TC = 16
BF = jnp.bfloat16
F32 = jnp.float32
MESH = pl.DeviceIdType.MESH


def split_np(a):
    hi = a.astype(jnp.bfloat16)
    lo = (a - hi.astype(np.float64)).astype(jnp.bfloat16)
    return hi, lo


def tables():
    p = np.arange(32)
    s = np.arange(TB)
    ang = 2.0 * np.pi * (np.outer(p, p) % 32) / 32
    first = np.concatenate([np.cos(ang), -np.sin(ang)], 0)
    hi, lo = split_np(first)
    first = np.concatenate([hi, hi, lo], 1)
    first = np.concatenate([first, np.zeros((64, 32), first.dtype)], 1)
    mid = 2.0 * np.pi * np.outer(p, s) / NT
    twiddle = np.concatenate([np.cos(mid), np.sin(mid)]).astype(np.float32)
    q = KLO // 32 + np.arange(NB // 32)
    ang = 2.0 * np.pi * (np.outer(q, s) % TB) / TB
    c, z = np.cos(ang), np.sin(ang)
    second = np.concatenate([np.concatenate([c, z], 1), np.concatenate([-z, c], 1)], 0)
    hi, lo = split_np(second)
    second = np.concatenate([hi, hi, lo], 1)
    return first, twiddle, second


def split(a):
    hi = a.astype(BF)
    lo = (a - hi.astype(F32)).astype(BF)
    return hi, lo


def kernel(
    raw, owner_in, slot_in, weight_in, first_in, twiddle_in, second_in, taper_in, out,
    owner, slot, weight, first, twiddle, second, taper, scale,
    blocks, codes, acc, sums, parts, rows, samples, mid, outgo, arrived,
    send_raw, recv_raw, send_code, recv_code, send_x, recv_x,
    send_t, recv_t, send_f, recv_f, index_sem, table_sem, own_sem, ring_sem,
):
    me = lax.axis_index("tm")
    g = lax.axis_index("chan")
    core, x, zl = lax.rem(g, 2), lax.rem(g // 2, NX), g // 8
    y, zh = lax.rem(me, 8), me // 8

    index_copies = [
        pltpu.make_async_copy(a, b, index_sem.at[k])
        for k, (a, b) in enumerate([(owner_in, owner), (slot_in, slot), (weight_in, weight)])
    ]
    table_copies = [
        pltpu.make_async_copy(a, b, table_sem.at[k])
        for k, (a, b) in enumerate(
            [(taper_in, taper), (first_in, first), (twiddle_in, twiddle), (second_in, second)]
        )
    ]
    for copy in index_copies:
        copy.start()

    def relative(k):
        n = k - 4
        if isinstance(k, int):
            return (n // 2 % 2, 1 + 2 * (n % 2), n // 4) if 4 <= k < 12 else (k // 2 % 2, 2 * (k // 12), k % 2)
        mid = (k >= 4) & (k < 12)
        dx = jnp.where(mid, 1 + 2 * lax.rem(k, 2), 2 * (k // 12))
        dz = lax.rem(k // 2, 2)
        dc = jnp.where(mid, n // 4, lax.rem(k, 2))
        return dz, dx, dc

    def to_chan(k):
        dz, dx, dc = relative(k)
        return (lax.rem(zl + dz, 2) * NX + lax.rem(x + dx, NX)) * 2 + lax.rem(core + dc, 2)

    def from_chan(k):
        dz, dx, dc = relative(k)
        return (lax.rem(zl + dz, 2) * NX + lax.rem(x + NX - dx, NX)) * 2 + lax.rem(core + dc, 2)

    def place_of(chan):
        dz = lax.rem(chan // 8 + zl, 2)
        dx = lax.rem(x + NX - (chan // 2) % NX, NX)
        dc = lax.rem(chan % 2 + core, 2)
        straight = 6 * dx + dz * 2 + dc
        return jnp.where(lax.rem(dx, 2) == 0, straight, 4 + dc * 4 + dz * 2 + dx // 2)

    def to_tm(n):
        if isinstance(n, int):
            dy, dz = (4, 3, 5, 2, 6, 1, 7, 0)[n // 4], (2, 1, 3, 0)[n % 4]
            return lax.rem(zh + dz, 4) * 8 + lax.rem(y + dy, 8)
        far, m = n // 4, lax.rem(n, 4)
        dy = 4 + jnp.where(lax.rem(far, 2) == 1, -((far + 1) // 2), far // 2)
        dz = jnp.where(m == 0, 2, jnp.where(m == 1, 1, jnp.where(m == 2, 3, 0)))
        return lax.rem(zh + dz, 4) * 8 + lax.rem(y + dy, 8)

    barrier = pltpu.get_barrier_semaphore()

    def along_y(d):
        return zh * 8 + lax.rem(y + d, 8)

    def greet_y(d, _):
        pl.semaphore_signal(barrier, inc=1, device_id=(along_y(d), g), device_id_type=MESH)
        return 0

    def greet_z(d, _):
        to = lax.rem(zh + d, 4) * 8 + y
        pl.semaphore_signal(barrier, inc=1, device_id=(to, g), device_id_type=MESH)
        return 0

    def tell_y(d, _):
        pl.semaphore_signal(ring_sem, inc=1, device_id=(along_y(d), g), device_id_type=MESH)
        return 0

    def greet_chan(k, _):
        pl.semaphore_signal(barrier, inc=1, device_id=(me, to_chan(k)), device_id_type=MESH)
        return 0

    lax.fori_loop(1, 8, greet_y, 0)
    lax.fori_loop(1, 4, greet_z, 0)
    lax.fori_loop(1, N_CHAN, greet_chan, 0)

    def chunk(i):
        return pl.ds(pl.multiple_of(i * TC, TC), TC)

    own_raw = pltpu.make_async_copy(raw.at[chunk(g), :], blocks.at[g], own_sem)
    own_raw.start()
    for copy in index_copies:
        copy.wait()
    code = (owner[...] * 256 + slot[...]) * 128 + weight[...]
    for j in range(2):
        for m in range(CH // 128):
            r = 6 * j + m
            codes[g, r // 4, pl.ds(r % 4, 1), :] = code[j : j + 1, 128 * m : 128 * m + 128]
    acc[...] = jnp.zeros_like(acc)
    pl.semaphore_wait(barrier, 7 + 3 + N_CHAN - 1)

    def raw_copy(k):
        to = to_chan(k)
        return pltpu.make_async_remote_copy(
            src_ref=raw.at[chunk(to), :], dst_ref=blocks.at[g],
            send_sem=send_raw.at[k], recv_sem=recv_raw.at[k],
            device_id=(me, to), device_id_type=MESH,
        )

    def code_copy(k):
        return pltpu.make_async_remote_copy(
            src_ref=codes.at[g], dst_ref=codes.at[g],
            send_sem=send_code.at[k], recv_sem=recv_code.at[k],
            device_id=(me, to_chan(k)), device_id_type=MESH,
        )

    def send_group(n, _):
        k = n + 1
        code_copy(k).start()
        raw_copy(k).start()
        return 0

    for n in range(N_CHAN - 1):
        send_group(n, 0)
    lax.fori_loop(1, 8, tell_y, 0)
    for copy in table_copies:
        copy.start()

    row = lax.broadcasted_iota(jnp.int32, (256, 128), 0).astype(F32).astype(BF)

    def process(src):
        total = None
        for m2 in range(CH // 256):
            data = [blocks[src, :, pl.ds(256 * m2 + 128 * n, 128)] for n in range(2)]
            for j in range(2):
                left, right = [], []
                for n in range(2):
                    r = 6 * j + 2 * m2 + n
                    c = codes[src, r // 4, pl.ds(r % 4, 1), :]

                    def spread(v):
                        return jnp.broadcast_to(v.astype(F32), (16, 128)).astype(BF)

                    key = spread(((c >> 15) << 4) + ((c >> 7) & 15))
                    low = spread(((c >> 11) & 1) * 8 + ((c >> 12) & 7))
                    w = spread(c & 127)
                    key = jnp.concatenate([key] * 16, 0)
                    w = jnp.concatenate([w] * 16, 0)
                    left.append(jnp.where(row == key, w, BF(0)))
                    right.append(
                        jnp.concatenate(
                            [jnp.where(low == BF(v), data[n], BF(0)) for v in range(16)], 0
                        )
                    )
                part = lax.dot_general(
                    jnp.concatenate(left, 1), jnp.concatenate(right, 1),
                    (((1,), (1,)), ((), ())), preferred_element_type=F32,
                )
                total = part if total is None else total + part
        acc[...] += total

    own_raw.wait()
    process(g)

    def step(k, _):
        code_copy(k).wait_recv()
        raw_copy(k).wait_recv()
        process(from_chan(k))
        return 0

    lax.fori_loop(1, N_CHAN, step, 0)
    for h in range(2):
        sums[:, pl.ds(16 * h, 16), :] = acc[:, pl.ds(128 * h, 128)].reshape(16, 16, 128)

    def part(i):
        return pl.ds(pl.multiple_of(i * 32, 32), 32)

    def x_copy(k):
        to = to_chan(k)
        return pltpu.make_async_remote_copy(
            src_ref=sums.at[to], dst_ref=parts.at[part(k), :],
            send_sem=send_x.at[k], recv_sem=recv_x.at[k],
            device_id=(me, to), device_id_type=MESH,
        )

    def send_part(n, _):
        x_copy(n + 1).start()
        return 0

    def wait_part(k, _):
        x_copy(k).wait_recv()
        return 0

    for n in range(N_CHAN - 1):
        send_part(n, 0)
    parts[pl.ds(0, 32), :] = sums[g]
    for copy in table_copies:
        copy.wait()
    quarter = lax.broadcasted_iota(jnp.int32, (8, 128), 1) // 32
    t = taper[...] * (1.0 / math.sqrt(NT))
    for j in range(4):
        line = jnp.zeros((8, 128), F32)
        for n in range(4):
            moved = pltpu.roll(t, (32 * (n - j)) % 128, 1) if n != j else t
            line = jnp.where(quarter == n, moved, line)
        scale[pl.ds(j, 8, 4), :] = line
    every = codes[...].reshape(N_CHAN * 3, 4, 128)
    inverse = []
    for b in range(8):
        hit = jnp.where((every >> 7) == g * 256 + b * 32 + me, every & 127, 0)
        total = jnp.sum(hit, axis=0).astype(F32)
        total = jnp.sum(jnp.sum(total, axis=0, keepdims=True), axis=1, keepdims=True)
        inverse.append(1.0 / jnp.maximum(total, 1.0))

    def send_rows(half):
        def send(n, _):
            to = to_tm(n)
            rows[to, pl.ds(8 * half, 8), :] = parts[pl.ds(256 * half + to, 8, 32), :]
            pltpu.make_async_remote_copy(
                src_ref=rows.at[to, pl.ds(8 * half, 8), :],
                dst_ref=samples.at[pl.ds(pl.multiple_of(me * 16 + 8 * half, 8), 8), :],
                send_sem=send_t, recv_sem=recv_t, device_id=(to, g), device_id_type=MESH,
            ).start()
            return 0

        for n in range(N_TM - 1):
            send(n, 0)

    pl.semaphore_wait(ring_sem, 7)
    for half in range(2):
        for k in range(max(1, 8 * half), 8 * half + 8):
            wait_part(k, 0)
        send_rows(half)
    samples[chunk(me), :] = parts[pl.ds(me, 16, 32), :]
    all_t = pltpu.make_async_remote_copy(
        src_ref=samples.at[pl.ds(0, 16 * (N_TM - 1)), :],
        dst_ref=samples.at[pl.ds(0, 16 * (N_TM - 1)), :],
        send_sem=send_t, recv_sem=recv_t, device_id=(to_tm(0), g), device_id_type=MESH,
    )
    all_t.wait_recv()

    lane = lax.broadcasted_iota(jnp.int32, (N_TM, 128), 1) // 16
    halves = []
    for u in range(2):
        v = [samples[pl.ds(place_of(8 * u + n), N_TM, 16), :] for n in range(8)]
        for bit in (1, 2, 4):
            low = (lane & bit) == 0
            w = list(v)
            for n in range(8):
                if n & bit == 0:
                    w[n] = jnp.where(low, v[n], pltpu.roll(v[n + bit], 16 * bit, 1))
                    w[n + bit] = jnp.where(low, pltpu.roll(v[n], 128 - 16 * bit, 1), v[n + bit])
            v = w
        halves.append(v)
    cos, sin = twiddle[pl.ds(0, 32), :], twiddle[pl.ds(32, 32), :]
    for b in range(8):
        hi, lo = split(jnp.concatenate([halves[0][b], halves[1][b]], 1) * inverse[b])
        here = jnp.concatenate([hi, lo, hi, jnp.zeros_like(hi)], 0)
        f = jnp.dot(first[...], here, preferred_element_type=F32)
        re, im = f[:32], f[32:]
        z = jnp.concatenate([re * cos + im * sin, im * cos - re * sin], 1)
        hi, lo = split(z)
        mid[pl.ds(32 * b, 32), pl.ds(0, 512)] = hi
        mid[pl.ds(32 * b, 32), pl.ds(512, 512)] = lo
        mid[pl.ds(32 * b, 32), pl.ds(1024, 512)] = hi
    spec = lax.dot_general(
        second[...], mid[...], (((1,), (1,)), ((), ())), preferred_element_type=F32
    )
    for r in range(2):
        for h in range(2):
            band = spec[32 * r : 32 * r + 32, 128 * h : 128 * h + 128] * scale[...]
            outgo[:, 2 * r + h, :] = band

    def send_band(n, _):
        to = to_tm(n)
        pltpu.make_async_remote_copy(
            src_ref=outgo.at[to], dst_ref=arrived.at[me],
            send_sem=send_f, recv_sem=recv_f, device_id=(to, g), device_id_type=MESH,
        ).start()
        return 0

    for n in range(N_TM - 1):
        send_band(n, 0)
    arrived[me] = outgo[me]
    all_f = pltpu.make_async_remote_copy(
        src_ref=arrived.at[pl.ds(0, N_TM - 1)], dst_ref=arrived.at[pl.ds(0, N_TM - 1)],
        send_sem=send_f, recv_sem=recv_f, device_id=(to_tm(0), g), device_id_type=MESH,
    )
    all_f.wait_recv()
    for r in range(2):
        for h in range(2):
            turned = arrived[:, 2 * r + h, :].T
            out[r, :, pl.ds(128 * h, 128)] = jnp.concatenate(
                [turned[32 * n : 32 * n + 32] for n in range(4)], 1
            )

    def drain(k, _):
        code_copy(k).wait_send()
        raw_copy(k).wait_send()
        x_copy(k).wait_send()
        return 0

    lax.fori_loop(1, N_CHAN, drain, 0)
    all_t.wait_send()
    all_f.wait_send()


def local(raw, taper, depth_owner, depth_slot, intersection):
    first, twiddle, second = tables()
    anywhere = pl.BlockSpec(memory_space=pl.ANY)
    dma = pltpu.SemaphoreType.DMA
    vmem = pltpu.VMEM
    got = pl.pallas_call(
        kernel,
        out_shape=jax.ShapeDtypeStruct((2, 32, 256), F32),
        in_specs=[anywhere] * 8,
        out_specs=pl.BlockSpec(memory_space=pltpu.VMEM),
        scratch_shapes=[
            vmem((2, CH), jnp.int32),
            vmem((2, CH), jnp.int32),
            vmem((2, CH), jnp.int32),
            vmem((64, 128), BF),
            vmem((64, TB), F32),
            vmem((64, 1536), BF),
            vmem((8, 128), F32),
            vmem((32, 128), F32),
            vmem((N_CHAN, TC, CH), BF),
            vmem((N_CHAN, 3, 4, 128), jnp.int32),
            vmem((256, 256), F32),
            vmem((N_CHAN, 32, 128), F32),
            vmem((N_CHAN * 32, 128), F32),
            vmem((N_TM, 16, 128), F32),
            vmem((N_TM * 16, 128), F32),
            vmem((256, 1536), BF),
            vmem((N_TM, 4, 128), F32),
            vmem((N_TM, 4, 128), F32),
        ]
        + [dma((N_CHAN,))] * 6
        + [dma, dma, dma, dma, dma((3,)), dma((4,)), dma, pltpu.SemaphoreType.REGULAR],
        compiler_params=pltpu.CompilerParams(
            collective_id=0, has_side_effects=True, vmem_limit_bytes=60 * 2**20
        ),
        name="stack_and_transform",
    )(
        raw, depth_owner.T, depth_slot.T, intersection.T,
        jnp.asarray(first), jnp.asarray(twiddle), jnp.asarray(second), taper.reshape(8, 128),
    )
    return got.transpose(0, 2, 1)


def solution(mesh):
    return jax.shard_map(
        local,
        mesh=mesh,
        in_specs=(P("tm", "chan"), P(), P("chan", None), P("chan", None), P("chan", None)),
        out_specs=P(None, "chan", "tm"),
        check_vma=False,
    )
```

```python
import math

import jax
import jax.numpy as jnp
import numpy as np
from jax import lax
from jax.experimental import pallas as pl
from jax.experimental.pallas import tpu as pltpu
from jax.sharding import PartitionSpec as P

NT = 8192
KLO = 128
NB = 1024
N_TM = 32
N_CHAN = 16
NX = 4
CH = 768
TB = 256
TC = 16
BF = jnp.bfloat16
F32 = jnp.float32
MESH = pl.DeviceIdType.MESH


def split_np(a):
    hi = a.astype(jnp.bfloat16)
    lo = (a - hi.astype(np.float64)).astype(jnp.bfloat16)
    return hi, lo


def tables():
    p = np.arange(32)
    s = np.arange(TB)
    ang = 2.0 * np.pi * (np.outer(p, p) % 32) / 32
    first = np.concatenate([np.cos(ang), -np.sin(ang)], 0)
    hi, lo = split_np(first)
    first = np.concatenate([hi, hi, lo], 1)
    first = np.concatenate([first, np.zeros((64, 32), first.dtype)], 1)
    mid = 2.0 * np.pi * np.outer(p, s) / NT
    twiddle = np.concatenate([np.cos(mid), np.sin(mid)]).astype(np.float32)
    q = KLO // 32 + np.arange(NB // 32)
    ang = 2.0 * np.pi * (np.outer(q, s) % TB) / TB
    c, z = np.cos(ang), np.sin(ang)
    second = np.concatenate([np.concatenate([c, z], 1), np.concatenate([-z, c], 1)], 0)
    hi, lo = split_np(second)
    second = np.concatenate([hi, hi, lo], 1)
    return first, twiddle, second


def split(a):
    hi = a.astype(BF)
    lo = (a - hi.astype(F32)).astype(BF)
    return hi, lo


def kernel(
    raw, owner_in, slot_in, weight_in, first_in, twiddle_in, second_in, taper_in, out,
    owner, slot, weight, first, twiddle, second, taper, scale,
    blocks, codes, acc, sums, parts, rows, samples, mid, outgo, arrived,
    send_raw, recv_raw, send_code, recv_code, send_x, recv_x,
    send_t, recv_t, send_f, recv_f, index_sem, table_sem, own_sem, ring_sem,
):
    me = lax.axis_index("tm")
    g = lax.axis_index("chan")
    core, x, zl = lax.rem(g, 2), lax.rem(g // 2, NX), g // 8
    y, zh = lax.rem(me, 8), me // 8

    index_copies = [
        pltpu.make_async_copy(a, b, index_sem.at[k])
        for k, (a, b) in enumerate([(owner_in, owner), (slot_in, slot), (weight_in, weight)])
    ]
    table_copies = [
        pltpu.make_async_copy(a, b, table_sem.at[k])
        for k, (a, b) in enumerate(
            [(taper_in, taper), (first_in, first), (twiddle_in, twiddle), (second_in, second)]
        )
    ]
    for copy in index_copies:
        copy.start()

    def relative(k):
        n = k - 4
        if isinstance(k, int):
            return (n // 2 % 2, 1 + 2 * (n % 2), n // 4) if 4 <= k < 12 else (k // 2 % 2, 2 * (k // 12), k % 2)
        mid = (k >= 4) & (k < 12)
        dx = jnp.where(mid, 1 + 2 * lax.rem(k, 2), 2 * (k // 12))
        dz = lax.rem(k // 2, 2)
        dc = jnp.where(mid, n // 4, lax.rem(k, 2))
        return dz, dx, dc

    def to_chan(k):
        dz, dx, dc = relative(k)
        return (lax.rem(zl + dz, 2) * NX + lax.rem(x + dx, NX)) * 2 + lax.rem(core + dc, 2)

    def from_chan(k):
        dz, dx, dc = relative(k)
        return (lax.rem(zl + dz, 2) * NX + lax.rem(x + NX - dx, NX)) * 2 + lax.rem(core + dc, 2)

    def place_of(chan):
        dz = lax.rem(chan // 8 + zl, 2)
        dx = lax.rem(x + NX - (chan // 2) % NX, NX)
        dc = lax.rem(chan % 2 + core, 2)
        straight = 6 * dx + dz * 2 + dc
        return jnp.where(lax.rem(dx, 2) == 0, straight, 4 + dc * 4 + dz * 2 + dx // 2)

    def to_tm(n):
        if isinstance(n, int):
            dy, dz = (4, 3, 5, 2, 6, 1, 7, 0)[n // 4], (2, 1, 3, 0)[n % 4]
            return lax.rem(zh + dz, 4) * 8 + lax.rem(y + dy, 8)
        far, m = n // 4, lax.rem(n, 4)
        dy = 4 + jnp.where(lax.rem(far, 2) == 1, -((far + 1) // 2), far // 2)
        dz = jnp.where(m == 0, 2, jnp.where(m == 1, 1, jnp.where(m == 2, 3, 0)))
        return lax.rem(zh + dz, 4) * 8 + lax.rem(y + dy, 8)

    barrier = pltpu.get_barrier_semaphore()

    def along_y(d):
        return zh * 8 + lax.rem(y + d, 8)

    def greet_y(d, _):
        pl.semaphore_signal(barrier, inc=1, device_id=(along_y(d), g), device_id_type=MESH)
        return 0

    def greet_z(d, _):
        to = lax.rem(zh + d, 4) * 8 + y
        pl.semaphore_signal(barrier, inc=1, device_id=(to, g), device_id_type=MESH)
        return 0

    def tell_y(d, _):
        pl.semaphore_signal(ring_sem, inc=1, device_id=(along_y(d), g), device_id_type=MESH)
        return 0

    def greet_chan(k, _):
        pl.semaphore_signal(barrier, inc=1, device_id=(me, to_chan(k)), device_id_type=MESH)
        return 0

    for d in range(1, 8):
        greet_y(d, 0)
    for d in range(1, 4):
        greet_z(d, 0)
    for d in range(1, N_CHAN):
        greet_chan(d, 0)

    def chunk(i):
        return pl.ds(pl.multiple_of(i * TC, TC), TC)

    own_raw = pltpu.make_async_copy(raw.at[chunk(g), :], blocks.at[g], own_sem)
    own_raw.start()
    for copy in index_copies:
        copy.wait()
    code = (owner[...] * 256 + slot[...]) * 128 + weight[...]
    for j in range(2):
        for m in range(CH // 128):
            r = 6 * j + m
            codes[g, r // 4, pl.ds(r % 4, 1), :] = code[j : j + 1, 128 * m : 128 * m + 128]
    acc[...] = jnp.zeros_like(acc)
    pl.semaphore_wait(barrier, 7 + 3 + N_CHAN - 1)

    def raw_copy(k):
        to = to_chan(k)
        return pltpu.make_async_remote_copy(
            src_ref=raw.at[chunk(to), :], dst_ref=blocks.at[g],
            send_sem=send_raw.at[k], recv_sem=recv_raw.at[k],
            device_id=(me, to), device_id_type=MESH,
        )

    def code_copy(k):
        return pltpu.make_async_remote_copy(
            src_ref=codes.at[g], dst_ref=codes.at[g],
            send_sem=send_code.at[k], recv_sem=recv_code.at[k],
            device_id=(me, to_chan(k)), device_id_type=MESH,
        )

    def send_group(n, _):
        k = n + 1
        code_copy(k).start()
        raw_copy(k).start()
        return 0

    for n in range(N_CHAN - 1):
        send_group(n, 0)
    for d in range(1, 8):
        tell_y(d, 0)
    for copy in table_copies:
        copy.start()

    row = lax.broadcasted_iota(jnp.int32, (256, 128), 0).astype(F32).astype(BF)

    def process(src):
        total = None
        for m2 in range(CH // 256):
            data = [blocks[src, :, pl.ds(256 * m2 + 128 * n, 128)] for n in range(2)]
            for j in range(2):
                left, right = [], []
                for n in range(2):
                    r = 6 * j + 2 * m2 + n
                    c = codes[src, r // 4, pl.ds(r % 4, 1), :]

                    def spread(v):
                        return jnp.broadcast_to(v.astype(F32), (16, 128)).astype(BF)

                    key = spread(((c >> 15) << 4) + ((c >> 7) & 15))
                    low = spread(((c >> 11) & 1) * 8 + ((c >> 12) & 7))
                    w = spread(c & 127)
                    key = jnp.concatenate([key] * 16, 0)
                    w = jnp.concatenate([w] * 16, 0)
                    left.append(jnp.where(row == key, w, BF(0)))
                    right.append(
                        jnp.concatenate(
                            [jnp.where(low == BF(v), data[n], BF(0)) for v in range(16)], 0
                        )
                    )
                part = lax.dot_general(
                    jnp.concatenate(left, 1), jnp.concatenate(right, 1),
                    (((1,), (1,)), ((), ())), preferred_element_type=F32,
                )
                total = part if total is None else total + part
        acc[...] += total

    own_raw.wait()
    process(g)

    def step(k, _):
        code_copy(k).wait_recv()
        raw_copy(k).wait_recv()
        process(from_chan(k))
        return 0

    lax.fori_loop(1, N_CHAN, step, 0)
    for h in range(2):
        sums[:, pl.ds(16 * h, 16), :] = acc[:, pl.ds(128 * h, 128)].reshape(16, 16, 128)

    def part(i):
        return pl.ds(pl.multiple_of(i * 32, 32), 32)

    def x_copy(k):
        to = to_chan(k)
        return pltpu.make_async_remote_copy(
            src_ref=sums.at[to], dst_ref=parts.at[part(k), :],
            send_sem=send_x.at[k], recv_sem=recv_x.at[k],
            device_id=(me, to), device_id_type=MESH,
        )

    def send_part(n, _):
        x_copy(n + 1).start()
        return 0

    def wait_part(k, _):
        x_copy(k).wait_recv()
        return 0

    for n in range(N_CHAN - 1):
        send_part(n, 0)
    parts[pl.ds(0, 32), :] = sums[g]
    for copy in table_copies:
        copy.wait()
    quarter = lax.broadcasted_iota(jnp.int32, (8, 128), 1) // 32
    t = taper[...] * (1.0 / math.sqrt(NT))
    for j in range(4):
        line = jnp.zeros((8, 128), F32)
        for n in range(4):
            moved = pltpu.roll(t, (32 * (n - j)) % 128, 1) if n != j else t
            line = jnp.where(quarter == n, moved, line)
        scale[pl.ds(j, 8, 4), :] = line
    every = codes[...].reshape(N_CHAN * 3, 4, 128)
    inverse = []
    for b in range(8):
        hit = jnp.where((every >> 7) == g * 256 + b * 32 + me, every & 127, 0)
        total = jnp.sum(hit, axis=0).astype(F32)
        total = jnp.sum(jnp.sum(total, axis=0, keepdims=True), axis=1, keepdims=True)
        inverse.append(1.0 / jnp.maximum(total, 1.0))

    def send_rows(half):
        def send(n, _):
            to = to_tm(n)
            rows[to, pl.ds(8 * half, 8), :] = parts[pl.ds(256 * half + to, 8, 32), :]
            pltpu.make_async_remote_copy(
                src_ref=rows.at[to, pl.ds(8 * half, 8), :],
                dst_ref=samples.at[pl.ds(pl.multiple_of(me * 16 + 8 * half, 8), 8), :],
                send_sem=send_t, recv_sem=recv_t, device_id=(to, g), device_id_type=MESH,
            ).start()
            return 0

        for n in range(N_TM - 1):
            send(n, 0)

    pl.semaphore_wait(ring_sem, 7)
    for half in range(2):
        for k in range(max(1, 8 * half), 8 * half + 8):
            wait_part(k, 0)
        send_rows(half)
    samples[chunk(me), :] = parts[pl.ds(me, 16, 32), :]
    all_t = pltpu.make_async_remote_copy(
        src_ref=samples.at[pl.ds(0, 16 * (N_TM - 1)), :],
        dst_ref=samples.at[pl.ds(0, 16 * (N_TM - 1)), :],
        send_sem=send_t, recv_sem=recv_t, device_id=(to_tm(0), g), device_id_type=MESH,
    )
    all_t.wait_recv()

    lane = lax.broadcasted_iota(jnp.int32, (N_TM, 128), 1) // 16
    halves = []
    for u in range(2):
        v = [samples[pl.ds(place_of(8 * u + n), N_TM, 16), :] for n in range(8)]
        for bit in (1, 2, 4):
            low = (lane & bit) == 0
            w = list(v)
            for n in range(8):
                if n & bit == 0:
                    w[n] = jnp.where(low, v[n], pltpu.roll(v[n + bit], 16 * bit, 1))
                    w[n + bit] = jnp.where(low, pltpu.roll(v[n], 128 - 16 * bit, 1), v[n + bit])
            v = w
        halves.append(v)
    cos, sin = twiddle[pl.ds(0, 32), :], twiddle[pl.ds(32, 32), :]
    for b in range(8):
        hi, lo = split(jnp.concatenate([halves[0][b], halves[1][b]], 1) * inverse[b])
        here = jnp.concatenate([hi, lo, hi, jnp.zeros_like(hi)], 0)
        f = jnp.dot(first[...], here, preferred_element_type=F32)
        re, im = f[:32], f[32:]
        z = jnp.concatenate([re * cos + im * sin, im * cos - re * sin], 1)
        hi, lo = split(z)
        mid[pl.ds(32 * b, 32), pl.ds(0, 512)] = hi
        mid[pl.ds(32 * b, 32), pl.ds(512, 512)] = lo
        mid[pl.ds(32 * b, 32), pl.ds(1024, 512)] = hi
    spec = lax.dot_general(
        second[...], mid[...], (((1,), (1,)), ((), ())), preferred_element_type=F32
    )
    for r in range(2):
        for h in range(2):
            band = spec[32 * r : 32 * r + 32, 128 * h : 128 * h + 128] * scale[...]
            outgo[:, 2 * r + h, :] = band

    def send_band(n, _):
        to = to_tm(n)
        pltpu.make_async_remote_copy(
            src_ref=outgo.at[to], dst_ref=arrived.at[me],
            send_sem=send_f, recv_sem=recv_f, device_id=(to, g), device_id_type=MESH,
        ).start()
        return 0

    for n in range(N_TM - 1):
        send_band(n, 0)
    arrived[me] = outgo[me]
    all_f = pltpu.make_async_remote_copy(
        src_ref=arrived.at[pl.ds(0, N_TM - 1)], dst_ref=arrived.at[pl.ds(0, N_TM - 1)],
        send_sem=send_f, recv_sem=recv_f, device_id=(to_tm(0), g), device_id_type=MESH,
    )
    def drain(k, _):
        code_copy(k).wait_send()
        raw_copy(k).wait_send()
        x_copy(k).wait_send()
        return 0

    lax.fori_loop(1, N_CHAN, drain, 0)
    all_t.wait_send()
    all_f.wait_recv()
    for r in range(2):
        for h in range(2):
            turned = arrived[:, 2 * r + h, :].T
            out[r, :, pl.ds(128 * h, 128)] = jnp.concatenate(
                [turned[32 * n : 32 * n + 32] for n in range(4)], 1
            )

    all_f.wait_send()


def local(raw, taper, depth_owner, depth_slot, intersection):
    first, twiddle, second = tables()
    anywhere = pl.BlockSpec(memory_space=pl.ANY)
    dma = pltpu.SemaphoreType.DMA
    vmem = pltpu.VMEM
    got = pl.pallas_call(
        kernel,
        out_shape=jax.ShapeDtypeStruct((2, 32, 256), F32),
        in_specs=[anywhere] * 8,
        out_specs=pl.BlockSpec(memory_space=pltpu.VMEM),
        scratch_shapes=[
            vmem((2, CH), jnp.int32),
            vmem((2, CH), jnp.int32),
            vmem((2, CH), jnp.int32),
            vmem((64, 128), BF),
            vmem((64, TB), F32),
            vmem((64, 1536), BF),
            vmem((8, 128), F32),
            vmem((32, 128), F32),
            vmem((N_CHAN, TC, CH), BF),
            vmem((N_CHAN, 3, 4, 128), jnp.int32),
            vmem((256, 256), F32),
            vmem((N_CHAN, 32, 128), F32),
            vmem((N_CHAN * 32, 128), F32),
            vmem((N_TM, 16, 128), F32),
            vmem((N_TM * 16, 128), F32),
            vmem((256, 1536), BF),
            vmem((N_TM, 4, 128), F32),
            vmem((N_TM, 4, 128), F32),
        ]
        + [dma((N_CHAN,))] * 6
        + [dma, dma, dma, dma, dma((3,)), dma((4,)), dma, pltpu.SemaphoreType.REGULAR],
        compiler_params=pltpu.CompilerParams(
            collective_id=0, has_side_effects=True, vmem_limit_bytes=60 * 2**20
        ),
        name="stack_and_transform",
    )(
        raw, depth_owner.T, depth_slot.T, intersection.T,
        jnp.asarray(first), jnp.asarray(twiddle), jnp.asarray(second), taper.reshape(8, 128),
    )
    return got.transpose(0, 2, 1)


def solution(mesh):
    return jax.shard_map(
        local,
        mesh=mesh,
        in_specs=(P("tm", "chan"), P(), P("chan", None), P("chan", None), P("chan", None)),
        out_specs=P(None, "chan", "tm"),
        check_vma=False,
    )
```
